32 devices in a mesh: group: 2 (over x), src: 16 (over z, y, core).
Axes of the slice: x: 2, y: 2, z: 4, core: 2. Of those that a mesh axis runs over, the one named last changes fastest.
Arguments:
- positions: float32 [2, 32768], P(None, ('group', 'src')), parts along dimension 1, may hold values from -0.2 to 0.2
- flux: float32 [4, 32768], P(None, ('group', 'src')), parts along dimension 1, may hold values from 0.1 to 2
- cluster: int32 [32768], P(('group', 'src')), parts along dimension 0, may hold values from 0 to 15
- jones: float32 [4, 2, 16, 1024], P(None, None, None, ('group', 'src')), parts along dimension 3, may hold values from -4 to 4
- station_uvw: float32 [3, 1024], P(None, ('group', 'src')), parts along dimension 1, may hold values from -600 to 600
- channels: int32 [8], P('group'), parts along dimension 0, may hold values from 0 to 383
- tile_map: int32 [32, 2], P('group'), parts along dimension 0, may hold values from 0 to 15, as said below
Outputs:
- visibilities: float32 [32, 4, 2, 1024], P(('group', 'src')), parts along dimension 0
The draws below stay inside these ranges and needn't reach their ends.
There are 2 independent parts, one for each index of `group`. The reference program is written for one: setup_inputs(seed, part) draws one part's arguments, and reference() takes and returns one part's arrays. A program takes and returns all parts, laid end to end along the dimension named above; each array names one. Nothing has to cross between parts.
Inputs may be any that keep to these rules, and one draw needn't show every extreme that they name: `tile_map`: each row is a pair of station tiles (first, second) with first <= second; the 16 pairs are distinct.
All inputs are finite; a program needn't handle non-finite values.
Results may differ from the reference program's by a relative error of at most 0.0038.
Values sent between devices are 32-bit elements; how exact they have to be, the bound alone decides.
No kernel may reach another device: no remote copies, remote signals or barrier semaphores. Data moves between devices by JAX's collectives and lax.ppermute only.
A program may use at most 128 MiB of HBM per device.

```python
import math
import jax
import jax.numpy as jnp
import numpy as np
from jax import lax

S = 512
C = 4
K = 16
TS = 32
SOURCES = 16384
BLOCKS = 16


def draw_tile_map(key, part):
    tiles = S // TS
    table = np.array([(first, second) for first in range(tiles) for second in range(first, tiles)], np.int32)
    count = table.shape[0]
    key_one, key_two = jax.random.split(jax.random.fold_in(key, 7))
    scores = jax.random.randint(key_one, (count,), 0, 1 << 20) * 256 + jnp.arange(count, dtype=jnp.int32)
    scores = scores.at[tiles - 1].set(1 << 29)
    order = jnp.argsort(-scores, stable=True)[:BLOCKS]
    shuffle = jax.random.permutation(key_two, BLOCKS)
    chosen = order[shuffle]
    return jnp.asarray(table)[chosen]


def place_ends(values, own_key, smallest, high):
    dims = values.shape
    index_at = [jax.random.randint(jax.random.fold_in(own_key, axis), (), 0, dims[axis]) for axis in range(len(dims))]
    values = values.at[tuple(index_at)].set(smallest)
    longest = dims.index(max(dims))
    index_at[longest] = (index_at[longest] + 1) % dims[longest]
    return values.at[tuple(index_at)].set(high)


def block_levels(own_key, dims, cuts, smallest, high):
    factor_of, own = 1.0, jax.random.fold_in(own_key, 6)
    for dim, parts in cuts:
        steps = jnp.exp(jax.random.uniform(jax.random.fold_in(own, dim), (parts,), jnp.float32, smallest / len(cuts), high / len(cuts)))
        factor_of = factor_of * jnp.repeat(steps, dims[dim] // parts).reshape([-1 if axis == dim else 1 for axis in range(len(dims))])
    return factor_of


def gaussian(rng, extent, spread, limit, cuts=(), held_as=jnp.bfloat16):
    gain = block_levels(rng, extent, cuts, -0.22, 0.18) if cuts else 1.0
    drawn = jax.random.normal(rng, extent, jnp.float32) * spread * gain
    return jnp.minimum(jnp.maximum(drawn, -limit), limit).astype(held_as)


def setup_inputs(seed: int = 0, part: int = 0) -> dict:
    splits = jax.random.split(jax.random.key(seed), 8)
    part_splits = jax.random.split(jax.random.fold_in(splits[7], part), 8)
    return {
        "positions": jnp.clip(jax.random.uniform(part_splits[0], (2, SOURCES), jnp.float32, -0.2, 0.2) * block_levels(part_splits[0], (2, SOURCES), ((1, 16),), -0.4, 0.0), -0.2, 0.2),
        "flux": jnp.clip(jnp.exp(math.log(2.0) - 2.9957323 * jax.random.uniform(part_splits[1], (C, SOURCES), jnp.float32) ** block_levels(part_splits[1], (C, SOURCES), ((1, 16),), -0.2, 0.2)), 0.1, 2.0),
        "cluster": place_ends(jax.random.randint(part_splits[2], (SOURCES,), 0, K), jax.random.fold_in(part_splits[2], 1), 0, K - 1).astype(jnp.int32),
        "jones": gaussian(part_splits[3], (C, 2, K, S), 0.7, 4.0, ((3, 16),), jnp.float32),
        "station_uvw": gaussian(part_splits[4], (3, S), 100.0, 600.0, ((1, 16),), jnp.float32),
        "channels": place_ends(jax.random.randint(part_splits[5], (C,), 0, 384), jax.random.fold_in(part_splits[5], 1), 0, 383).astype(jnp.int32),
        "tile_map": draw_tile_map(jax.random.fold_in(jax.random.fold_in(splits[7], part), 71), part),
    }


def phasors(station_gain, coords_uvw, coords, cluster_val, freq_ratio):
    directions = station_gain.shape[2]
    onehot = (cluster_val[None, :] == jnp.arange(directions, dtype=jnp.float32)[:, None]).astype(jnp.float32)
    gain_re = jnp.einsum('ckp,kn->cpn', station_gain[:, 0], onehot, precision=lax.Precision.HIGHEST)
    gain_im = jnp.einsum('ckp,kn->cpn', station_gain[:, 1], onehot, precision=lax.Precision.HIGHEST)
    l_term = coords[0]
    m_term = coords[1]
    n_term = jnp.sqrt(1.0 - l_term * l_term - m_term * m_term)
    argument = coords_uvw[0][:, None] * l_term[None, :] + coords_uvw[1][:, None] * m_term[None, :] + coords_uvw[2][:, None] * (n_term - 1.0)[None, :]
    phase = (2.0 * math.pi * freq_ratio)[:, None, None] * argument[None]
    cosine = jnp.cos(phase)
    sine = jnp.sin(phase)
    real_part = gain_re * cosine + gain_im * sine
    imag_part = gain_im * cosine - gain_re * sine
    return (real_part, imag_part)

def weighted_side(real_part, imag_part, fluxes, scale):
    weight = fluxes[:, None, :] * scale
    return jnp.stack([real_part * weight, imag_part * weight], 2).astype(jnp.bfloat16)

def plain_side(real_part, imag_part):
    return jnp.stack([real_part, imag_part], 2).astype(jnp.bfloat16)

def reference(positions, flux, cluster, jones, station_uvw, channels, tile_map):
    freq_ratio = 1.0 + 0.002 * channels.astype(jnp.float32)
    scale = 1.0 / math.sqrt(SOURCES)
    width = math.gcd(SOURCES, 4096)
    turns = SOURCES // width
    first_tile = tile_map[:, 0]
    second_tile = tile_map[:, 1]
    tiles = S // TS
    chans = jones.shape[0]

    def accumulate(total, turn):
        begin = (turn * width).astype(jnp.int32)
        coords = lax.dynamic_slice_in_dim(positions, begin, width, 1)
        fluxes = lax.dynamic_slice_in_dim(flux, begin, width, 1)
        cluster_val = lax.dynamic_slice_in_dim(cluster, begin, width, 0).astype(jnp.float32)
        real_part, imag_part = phasors(jones, station_uvw, coords, cluster_val, freq_ratio)
        weighted = weighted_side(real_part, imag_part, fluxes, scale).reshape(chans, tiles, TS, 2, width)
        plain = plain_side(real_part, imag_part).reshape(chans, tiles, TS, 2, width)
        left_sel = jnp.take(weighted, first_tile, axis=1).astype(jnp.float32)
        right_sel = jnp.take(plain, second_tile, axis=1).astype(jnp.float32)
        real_sum = jnp.einsum('cbirx,cbjrx->bcij', left_sel, right_sel)
        imag_sum = jnp.einsum('cbix,cbjx->bcij', left_sel[:, :, :, 1], right_sel[:, :, :, 0]) - jnp.einsum('cbix,cbjx->bcij', left_sel[:, :, :, 0], right_sel[:, :, :, 1])
        return (total + jnp.stack([real_sum, imag_sum], 2), None)
    blocks = tile_map.shape[0]
    start_total = jnp.zeros((blocks, chans, 2, TS, TS), jnp.float32)
    total, unused = lax.scan(accumulate, start_total, jnp.arange(turns, dtype=jnp.int32))
    same_tile = (first_tile == second_tile)[:, None, None, None, None]
    diagonal = (jnp.arange(TS)[:, None] == jnp.arange(TS)[None, :])[None, None, None]
    total = jnp.where(same_tile & diagonal, jnp.float32(0.0), total)
    return total.reshape(blocks, chans, 2, TS * TS)
```

```python
import functools
import math

import jax
import jax.numpy as jnp
from jax import lax
from jax.experimental import pallas as pl
from jax.experimental.pallas import tpu as pltpu
from jax.sharding import PartitionSpec as P

TS = 32
LANES = 128

A0, A1, A2, A3 = 3.1415628696601985, -5.166617869525222, 2.538088675224665, -0.546492984410238
B0, B1, B2 = A0 / A3, A1 / A3, A2 / A3
TOP = 1.0 / (A3 * A3)
GUARD = TOP * (1.0 + 1e-6)
SCALE = 2.0 * A3 * A3

ROWS_K = 128
GAIN_AT = 48


def split3(x):
    a = x.astype(jnp.bfloat16).astype(jnp.float32)
    b = (x - a).astype(jnp.bfloat16).astype(jnp.float32)
    return a, b, x - a - b


def station_rows(block):
    coords = block[0:8]
    re = block[8:24]
    im = block[24:40]
    turns = jnp.arctan2(im, re) * (-0.5 / math.pi)
    big = jnp.maximum(jnp.abs(re), jnp.abs(im))
    small = jnp.minimum(jnp.abs(re), jnp.abs(im))
    ratio = small / jnp.where(big == 0.0, 1.0, big)
    size = SCALE * big * jnp.sqrt(1.0 + ratio * ratio)
    u0, u1, u2 = split3(coords)
    t0, t1, t2 = split3(turns)
    g0, g1, g2 = split3(size)
    pad = jnp.zeros((ROWS_K - GAIN_AT - 48, block.shape[1]), jnp.float32)
    none = jnp.zeros((GAIN_AT, block.shape[1]), jnp.float32)
    phase = jnp.concatenate([u0, u0, u1, u0, u2, u1, t0, t1, t2, pad], 0)
    amplitude = jnp.concatenate([none, g0, g1, g2, pad], 0)
    return phase.T.astype(jnp.bfloat16), amplitude.T.astype(jnp.bfloat16)


def source_rows(src):
    s0, s1, s2 = split3(src)
    kinds = lax.broadcasted_iota(jnp.int32, (16, src.shape[1]), 0).astype(jnp.float32)
    onehot = jnp.where(src[3:4] == kinds, 1.0, 0.0)
    return jnp.concatenate([s0, s1, s0, s2, s0, s1, onehot, onehot, onehot], 0)


def phasor(turns, size):
    r = turns - lax.round(turns, lax.RoundingMethod.TO_NEAREST_EVEN)
    y = r * r
    s = r * (((y + B2) * y + B1) * y + B0)
    q = s * s
    rest = GUARD - q
    c = rest * lax.rsqrt(rest)
    return size * (0.5 * TOP - q), (size * s) * c


def tile_kernel(chans, shards, width, step, st_count, so_count, *refs):
    at_ref = refs[0]
    st_pieces = refs[1 : 1 + st_count]
    so_pieces = refs[1 + st_count : 1 + st_count + so_count]
    out_ref, st_buf, so_buf, lhs, rows, sides, total, st_sem, so_sem = refs[1 + st_count + so_count :]
    copies = []
    for pieces, buf, sem in ((st_pieces, st_buf, st_sem), (so_pieces, so_buf, so_sem)):
        begin = 0
        for n, piece in enumerate(pieces):
            size = piece.shape[0]
            copy = pltpu.make_async_copy(piece, buf.at[pl.ds(begin, size)], sem.at[n])
            copy.start()
            copies.append(copy)
            begin += size
    total[...] = jnp.zeros_like(total)
    rows[96:, :] = jnp.zeros((ROWS_K - 96, width), jnp.bfloat16)
    for copy in copies:
        copy.wait()
    for side in range(2):
        phase, amplitude = station_rows(st_buf[at_ref[side]])
        lhs[side * LANES : (side + 1) * LANES] = phase
        lhs[(2 + side) * LANES : (3 + side) * LANES] = amplitude

    def shard(i, carry):
        src = so_buf[i]
        rows[0:96, :] = source_rows(src).astype(jnp.bfloat16)
        for j in range(width // step):
            cut = slice(j * step, (j + 1) * step)
            both = jnp.dot(lhs[...], rows[:, cut], preferred_element_type=jnp.float32)
            for side in range(2):
                for c in range(chans):
                    at = (side * chans + c) * TS
                    turns = both[at : at + TS]
                    size = both[2 * LANES + at : 2 * LANES + at + TS]
                    if side == 0:
                        size = size * src[4 + c : 5 + c, cut]
                    re, im = phasor(turns, size)
                    sides[2 * at : 2 * at + TS, cut] = re.astype(jnp.bfloat16)
                    sides[2 * at + TS : 2 * at + 2 * TS, cut] = im.astype(jnp.bfloat16)
        for c in range(chans):
            left = sides[2 * c * TS : 2 * (c + 1) * TS]
            right = sides[2 * (chans + c) * TS : 2 * (chans + c + 1) * TS]
            total[c] += lax.dot_general(
                left, right, (((1,), (1,)), ((), ())), preferred_element_type=jnp.float32
            )
        return carry

    lax.fori_loop(0, shards, shard, 0)
    same = at_ref[2] == 1
    diagonal = lax.broadcasted_iota(jnp.int32, (TS, TS), 0) == lax.broadcasted_iota(jnp.int32, (TS, TS), 1)
    clear = jnp.logical_and(diagonal, same)
    for c in range(chans):
        whole = total[c]
        real = whole[:TS, :TS] + whole[TS:, TS:]
        imag = whole[TS:, :TS] - whole[:TS, TS:]
        out_ref[c, 0] = jnp.where(clear, 0.0, real)
        out_ref[c, 1] = jnp.where(clear, 0.0, imag)


def predict(at, stations, sources, chans):
    shards = sum(s.shape[0] for s in sources)
    width = sources[0].shape[2]
    step = math.gcd(width, 256)
    held = sum(s.shape[0] for s in stations)
    kernel = functools.partial(tile_kernel, chans, shards, width, step, len(stations), len(sources))
    count = len(stations) + len(sources)
    return pl.pallas_call(
        kernel,
        out_shape=jax.ShapeDtypeStruct((chans, 2, TS, TS), jnp.float32),
        in_specs=[pl.BlockSpec(memory_space=pltpu.SMEM)] + [pl.BlockSpec(memory_space=pl.ANY)] * count,
        out_specs=pl.BlockSpec(memory_space=pltpu.VMEM),
        scratch_shapes=[
            pltpu.VMEM((held,) + stations[0].shape[1:], jnp.float32),
            pltpu.VMEM((shards,) + sources[0].shape[1:], jnp.float32),
            pltpu.VMEM((4 * LANES, ROWS_K), jnp.bfloat16),
            pltpu.VMEM((ROWS_K, width), jnp.bfloat16),
            pltpu.VMEM((4 * chans * TS, width), jnp.bfloat16),
            pltpu.VMEM((chans, 2 * TS, 2 * TS), jnp.float32),
            pltpu.SemaphoreType.DMA((len(stations),)),
            pltpu.SemaphoreType.DMA((len(sources),)),
        ],
        compiler_params=pltpu.CompilerParams(vmem_limit_bytes=32 << 20),
    )(at, *stations, *sources)


def spread(parts, size):
    held = [[x] for x in parts]
    bit = size // 2
    while bit:
        pairs = [(i, i ^ bit) for i in range(size)]
        sent = [x[0] if len(x) == 1 else jnp.concatenate(x, 0) for x in held]
        for x, whole in zip(held, sent):
            x.append(lax.ppermute(whole, "src", pairs))
        bit //= 2
    return held


def place(mask, size):
    at, order, bit = 0 * mask, 0, size // 2
    while bit:
        at = at + ((mask // bit) % 2) * (1 << order)
        order, bit = order + 1, bit // 2
    return at


def on_device(positions, flux, cluster, jones, station_uvw, channels, tile_map):
    size = lax.axis_size("src")
    src_dev = positions.shape[1]
    chans, _, directions, own = jones.shape
    scale = 1.0 / math.sqrt(src_dev * size)
    freq_ratio = 1.0 + 0.002 * channels.astype(jnp.float32)
    n_term = jnp.sqrt(1.0 - positions[0] * positions[0] - positions[1] * positions[1]) - 1.0
    source = jnp.concatenate(
        [positions, n_term[None], cluster.astype(jnp.float32)[None], flux * scale], 0
    )[None]
    coords = station_uvw[:, None, :] * freq_ratio[None, :, None]
    gains = jnp.transpose(jones, (1, 2, 0, 3))
    station = jnp.concatenate(
        [
            coords.reshape(3, chans * own),
            jnp.zeros((5, chans * own), jnp.float32),
            gains.reshape(2 * directions, chans * own),
        ],
        0,
    )[None]
    stations, sources = spread([station, source], size)
    me = lax.axis_index("src")
    own_rows = tile_map.shape[0] // size
    many = TS // own
    out = []
    for row in range(own_rows):
        pair = lax.dynamic_slice_in_dim(tile_map, me * own_rows + row, 1, 0)[0]
        same = (pair[0] == pair[1]).astype(jnp.int32)
        if many == 1:
            at = jnp.stack([place(pair[0] ^ me, size), place(pair[1] ^ me, size), same])
            used = stations
        else:
            whole = jnp.concatenate(stations, 0)
            of = place((pair[:, None] * many + jnp.arange(many)[None, :]) ^ me, size)
            picked = jnp.take(whole, of.reshape(-1), axis=0)
            picked = picked.reshape(2, many, whole.shape[1], chans, own)
            picked = jnp.transpose(picked, (0, 2, 3, 1, 4)).reshape(2, whole.shape[1], chans * TS)
            used = [picked]
            at = jnp.stack([0 * same, 0 * same + 1, same])
        out.append(predict(at, used, sources, chans))
    return jnp.stack(out).reshape(own_rows, chans, 2, TS * TS)


def solution(mesh):
    in_specs = (
        P(None, ("group", "src")),
        P(None, ("group", "src")),
        P(("group", "src")),
        P(None, None, None, ("group", "src")),
        P(None, ("group", "src")),
        P("group"),
        P("group", None),
    )
    out_specs = P(("group", "src"), None, None, None)
    return jax.shard_map(
        on_device, mesh=mesh, in_specs=in_specs, out_specs=out_specs, check_vma=False
    )
```

```python
import functools
import math

import jax
import jax.numpy as jnp
from jax import lax
from jax.experimental import pallas as pl
from jax.experimental.pallas import tpu as pltpu
from jax.sharding import PartitionSpec as P

TS = 32
LANES = 128
STEP = 256

A0, A1, A2, A3 = 3.1415628696601985, -5.166617869525222, 2.538088675224665, -0.546492984410238
B0, B1, B2 = A0 / A3, A1 / A3, A2 / A3
TOP = 1.0 / (A3 * A3)
GUARD = TOP * (1.0 + 1e-6)
SCALE = 2.0 * A3 * A3

COORD_ROWS = 8
SOURCE_ROWS = 6 * COORD_ROWS


def split3(x):
    a = x.astype(jnp.bfloat16).astype(jnp.float32)
    b = (x - a).astype(jnp.bfloat16).astype(jnp.float32)
    return a, b, x - a - b


def station_rows(block, directions, depth):
    coords = block[:COORD_ROWS]
    re = block[COORD_ROWS : COORD_ROWS + directions]
    im = block[COORD_ROWS + directions :]
    turns = jnp.arctan2(im, re) * (-0.5 / math.pi)
    big = jnp.maximum(jnp.abs(re), jnp.abs(im))
    small = jnp.minimum(jnp.abs(re), jnp.abs(im))
    ratio = small / jnp.where(big == 0.0, 1.0, big)
    size = SCALE * big * jnp.sqrt(1.0 + ratio * ratio)
    u0, u1, u2 = split3(coords)
    t0, t1, t2 = split3(turns)
    g0, g1, g2 = split3(size)
    pad = jnp.zeros((depth - SOURCE_ROWS - 3 * directions, block.shape[1]), jnp.float32)
    none = jnp.zeros((SOURCE_ROWS, block.shape[1]), jnp.float32)
    phase = jnp.concatenate([u0, u0, u1, u0, u2, u1, t0, t1, t2, pad], 0)
    amplitude = jnp.concatenate([none, g0, g1, g2, pad], 0)
    return phase.T.astype(jnp.bfloat16), amplitude.T.astype(jnp.bfloat16)


def source_rows(src, directions, depth):
    s0, s1, s2 = split3(src)
    kinds = lax.broadcasted_iota(jnp.int32, (directions, src.shape[1]), 0).astype(jnp.float32)
    onehot = jnp.where(src[3:4] == kinds, 1.0, 0.0).astype(jnp.bfloat16)
    first = jnp.concatenate([s0, s1], 0).astype(jnp.bfloat16)
    second = jnp.concatenate([s0, s2], 0).astype(jnp.bfloat16)
    pad = jnp.zeros((depth - SOURCE_ROWS - 3 * directions, src.shape[1]), jnp.bfloat16)
    return jnp.concatenate([first, second, first, onehot, onehot, onehot, pad], 0)


def phasor(turns, size):
    r = turns - lax.round(turns, lax.RoundingMethod.TO_NEAREST_EVEN)
    y = r * r
    s = r * (((y + B2) * y + B1) * y + B0)
    q = s * s
    rest = GUARD - q
    c = rest * lax.rsqrt(rest)
    return size * (0.5 * TOP - q), (size * s) * c


def place(mask, size):
    at, order, bit = 0 * mask, 0, size // 2
    while bit:
        at = at + ((mask // bit) % 2) * (1 << order)
        order, bit = order + 1, bit // 2
    return at


def add_sources(chans, directions, depth, so_ref, lhs, total, both0, both1, sides0, sides1):
    shards, _, width = so_ref.shape
    step = math.gcd(width, STEP)
    per = width // step
    last = shards * per // 2
    sides1[...] = jnp.zeros_like(sides1)

    def part(t):
        return so_ref[t // per, :, pl.ds(pl.multiple_of(lax.rem(t, per) * step, step), step)]

    def product(t, into):
        made = source_rows(part(t), directions, depth)
        into[...] = jnp.dot(lhs[...], made, preferred_element_type=jnp.float32)

    def phasors(t, both, sides):
        weights = part(t)[4:]
        for side in range(2):
            for c in range(chans):
                at = (side * chans + c) * TS
                turns = both[at : at + TS]
                size = both[2 * LANES + at : 2 * LANES + at + TS]
                if side == 0:
                    size = size * weights[c : c + 1]
                re, im = phasor(turns, size)
                sides[2 * at : 2 * at + TS] = re.astype(jnp.bfloat16)
                sides[2 * at + TS : 2 * at + 2 * TS] = im.astype(jnp.bfloat16)

    def collect(sides):
        for at in range(0, 2 * chans * TS, LANES):
            total[at : at + LANES] += lax.dot_general(
                sides[at : at + LANES],
                sides[2 * chans * TS + at : 2 * chans * TS + at + LANES],
                (((1,), (1,)), ((), ())),
                preferred_element_type=jnp.float32,
            )

    product(0, both0)

    def turn(t, carry):
        product(last + t, both1)
        phasors(t, both0, sides0)
        collect(sides1)
        product(jnp.minimum(t + 1, last - 1), both0)
        phasors(last + t, both1, sides1)
        collect(sides0)
        return carry

    lax.fori_loop(0, last, turn, 0)
    collect(sides1)


def first_kernel(chans, directions, depth, row, size, pairs_ref, st0, st1, so_ref, lhs, total, *work):
    held = st0.shape[0]
    total[...] = jnp.zeros_like(total)
    for side in range(2):
        if row is None:
            at = side
        else:
            me = lax.axis_index("src")
            at = place(pairs_ref[me * row[0] + row[1], side] ^ me, size)
        low = lax.rem(at, held)
        block = jnp.where(at < held, st0[low], st1[low])
        phase, amplitude = station_rows(block, directions, depth)
        lhs[side * LANES : (side + 1) * LANES] = phase
        lhs[(2 + side) * LANES : (3 + side) * LANES] = amplitude
    add_sources(chans, directions, depth, so_ref, lhs, total, *work)


def next_kernel(chans, directions, depth, lhs, before, so_ref, total, *work):
    total[...] = before[...]
    add_sources(chans, directions, depth, so_ref, lhs, total, *work)


def last_kernel(chans, directions, depth, row, pairs_ref, lhs, before, so_ref, out_ref, total, *work):
    total[...] = before[...]
    add_sources(chans, directions, depth, so_ref, lhs, total, *work)
    me = lax.axis_index("src") * row[0] + row[1]
    same = pairs_ref[me, 0] == pairs_ref[me, 1]
    high = lax.broadcasted_iota(jnp.int32, (8, LANES), 0)
    lane = lax.broadcasted_iota(jnp.int32, (8, LANES), 1)
    fold = LANES // TS
    clear = jnp.logical_and(lane % TS == high * fold + lane // TS, same)
    for c in range(chans):
        base = 2 * c * TS
        column = base % LANES
        real = jnp.zeros((8, LANES), jnp.float32)
        imag = jnp.zeros((8, LANES), jnp.float32)
        for b in range(fold):
            w_re = total[pl.ds(base + b, 8, stride=fold)]
            w_im = total[pl.ds(base + TS + b, 8, stride=fold)]
            here = lane // TS == b
            one = (b * TS - column) % LANES
            two = (b * TS - column - TS) % LANES
            real = jnp.where(here, pltpu.roll(w_re, one, 1) + pltpu.roll(w_im, two, 1), real)
            imag = jnp.where(here, pltpu.roll(w_im, one, 1) - pltpu.roll(w_re, two, 1), imag)
        for n, values in enumerate((real, imag)):
            values = jnp.where(clear, 0.0, values)
            for m in range(8):
                out_ref[c, n : n + 1, m * LANES : (m + 1) * LANES] = values[m : m + 1]


class Predictor:
    def __init__(self, chans, directions, width):
        self.chans, self.directions = chans, directions
        self.depth = -(-(SOURCE_ROWS + 3 * directions) // LANES) * LANES
        step = math.gcd(width, STEP)
        self.work = [
            pltpu.VMEM((4 * LANES, step), jnp.float32),
            pltpu.VMEM((4 * LANES, step), jnp.float32),
            pltpu.VMEM((4 * chans * TS, step), jnp.bfloat16),
            pltpu.VMEM((4 * chans * TS, step), jnp.bfloat16),
        ]
        self.total = (2 * chans * TS, LANES)

    def call(self, kernel, out_shape, in_specs, scratch, args):
        vmem = pl.BlockSpec(memory_space=pltpu.VMEM)
        sources = args[-1].shape[0] * args[-1].shape[2]
        count = 2 * self.chans * TS * sources
        return pl.pallas_call(
            kernel,
            out_shape=out_shape,
            in_specs=in_specs + [vmem] * (len(args) - len(in_specs)),
            out_specs=jax.tree.map(lambda _: vmem, out_shape),
            scratch_shapes=scratch,
            compiler_params=pltpu.CompilerParams(vmem_limit_bytes=32 << 20),
            cost_estimate=pl.CostEstimate(flops=2000 * count, bytes_accessed=0, transcendentals=count),
        )(*args)

    def first(self, row, size, pairs, stations, sources):
        kernel = functools.partial(first_kernel, self.chans, self.directions, self.depth, row, size)
        shapes = (
            jax.ShapeDtypeStruct((4 * LANES, self.depth), jnp.bfloat16),
            jax.ShapeDtypeStruct(self.total, jnp.float32),
        )
        smem = pl.BlockSpec(memory_space=pltpu.SMEM)
        return self.call(kernel, shapes, [smem], self.work, (pairs, *stations, sources))

    def next(self, lhs, total, sources):
        kernel = functools.partial(next_kernel, self.chans, self.directions, self.depth)
        shape = jax.ShapeDtypeStruct(self.total, jnp.float32)
        return self.call(kernel, shape, [], self.work, (lhs, total, sources))

    def last(self, row, pairs, lhs, total, sources):
        kernel = functools.partial(last_kernel, self.chans, self.directions, self.depth, row)
        shape = jax.ShapeDtypeStruct((self.chans, 2, TS * TS), jnp.float32)
        smem = pl.BlockSpec(memory_space=pltpu.SMEM)
        scratch = [pltpu.VMEM(self.total, jnp.float32)] + self.work
        return self.call(kernel, shape, [smem], scratch, (pairs, lhs, total, sources))


def pack_kernel(scale, chans, channel_ref, positions_ref, flux_ref, cluster_ref, jones_ref, uvw_ref, station_ref, source_ref):
    own = uvw_ref.shape[1]
    directions = jones_ref.shape[2]
    coords = positions_ref[...]
    l_term, m_term = coords[0:1], coords[1:2]
    source_ref[0, 0:2] = coords
    source_ref[0, 2:3] = jnp.sqrt(1.0 - l_term * l_term - m_term * m_term) - 1.0
    source_ref[0, 3:4] = cluster_ref[...].astype(jnp.float32)
    source_ref[0, 4:] = flux_ref[...] * scale
    station_ref[...] = jnp.zeros_like(station_ref)
    for c in range(chans):
        lanes = slice(c * own, (c + 1) * own)
        ratio = 1.0 + 0.002 * channel_ref[c].astype(jnp.float32)
        station_ref[0, 0:3, lanes] = uvw_ref[...] * ratio
        for n in range(2):
            begin = COORD_ROWS + n * directions
            station_ref[0, begin : begin + directions, lanes] = jones_ref[c, n]


def pack(positions, flux, cluster, jones, station_uvw, channels, scale):
    chans, _, directions, own = jones.shape
    vmem = pl.BlockSpec(memory_space=pltpu.VMEM)
    return pl.pallas_call(
        functools.partial(pack_kernel, scale, chans),
        out_shape=(
            jax.ShapeDtypeStruct((1, COORD_ROWS + 2 * directions, chans * own), jnp.float32),
            jax.ShapeDtypeStruct((1, 4 + chans, positions.shape[1]), jnp.float32),
        ),
        in_specs=[pl.BlockSpec(memory_space=pltpu.SMEM)] + [vmem] * 5,
        out_specs=(vmem, vmem),
    )(channels, positions, flux, cluster[None], jones, station_uvw)


def swap(x, bit, size):
    return lax.ppermute(x, "src", [(i, i ^ bit) for i in range(size)])


def spread(station, size):
    bit = size // 2
    while bit:
        got = swap(station, bit, size)
        if bit > 1:
            station = jnp.concatenate([station, got], 0)
        bit //= 2
    return station, got


def on_device(positions, flux, cluster, jones, station_uvw, channels, tile_map):
    size = lax.axis_size("src")
    chans, _, directions, own = jones.shape
    scale = 1.0 / math.sqrt(positions.shape[1] * size)
    station, source = pack(positions, flux, cluster, jones, station_uvw, channels, scale)
    stations = spread(station, size)
    bit = size // 2
    while bit > 2:
        source = jnp.concatenate([source, swap(source, bit, size)], 0)
        bit //= 2
    own_rows = tile_map.shape[0] // size
    many = TS // own
    predictor = Predictor(chans, directions, positions.shape[1])
    begun = []
    for row in range(own_rows):
        if many == 1:
            begun.append(predictor.first((own_rows, row), size, tile_map, stations, source))
        else:
            me = lax.axis_index("src")
            pair = lax.dynamic_slice_in_dim(tile_map, me * own_rows + row, 1, 0)[0]
            whole = jnp.concatenate(stations, 0)
            of = place((pair[:, None] * many + jnp.arange(many)[None, :]) ^ me, size)
            picked = jnp.take(whole, of.reshape(-1), axis=0)
            picked = picked.reshape(2, many, whole.shape[1], chans, own)
            picked = jnp.transpose(picked, (0, 2, 3, 1, 4)).reshape(2, whole.shape[1], chans * TS)
            begun.append(predictor.first(None, size, tile_map, (picked, picked), source))
    got = swap(source, 2, size)
    both = jnp.concatenate([source, got], 0)
    other = swap(both, 1, size)
    out = []
    for row, (lhs, total) in enumerate(begun):
        total = predictor.next(lhs, total, got)
        out.append(predictor.last((own_rows, row), tile_map, lhs, total, other))
    return jnp.stack(out)


def solution(mesh):
    in_specs = (
        P(None, ("group", "src")),
        P(None, ("group", "src")),
        P(("group", "src")),
        P(None, None, None, ("group", "src")),
        P(None, ("group", "src")),
        P("group"),
        P("group", None),
    )
    out_specs = P(("group", "src"), None, None, None)
    return jax.shard_map(
        on_device, mesh=mesh, in_specs=in_specs, out_specs=out_specs, check_vma=False
    )
```

```python
import functools
import math

import jax
import jax.numpy as jnp
from jax import lax
from jax.experimental import pallas as pl
from jax.experimental.pallas import tpu as pltpu
from jax.sharding import PartitionSpec as P

TS = 32
LANES = 128
STEP = 256
WAYS = 16

A0, A1, A2, A3 = 3.1415628696601985, -5.166617869525222, 2.538088675224665, -0.546492984410238
B0, B1, B2 = A0 / A3, A1 / A3, A2 / A3
TOP = 1.0 / (A3 * A3)
GUARD = TOP * (1.0 + 1e-6)
SCALE = 2.0 * A3 * A3

COORD_ROWS = 8
SOURCE_ROWS = 6 * COORD_ROWS


def split3(x):
    a = x.astype(jnp.bfloat16).astype(jnp.float32)
    b = (x - a).astype(jnp.bfloat16).astype(jnp.float32)
    return a, b, x - a - b


def station_rows(block, directions, depth):
    coords = block[:COORD_ROWS]
    re = block[COORD_ROWS : COORD_ROWS + directions]
    im = block[COORD_ROWS + directions :]
    turns = jnp.arctan2(im, re) * (-0.5 / math.pi)
    big = jnp.maximum(jnp.abs(re), jnp.abs(im))
    small = jnp.minimum(jnp.abs(re), jnp.abs(im))
    ratio = small / jnp.where(big == 0.0, 1.0, big)
    size = SCALE * big * jnp.sqrt(1.0 + ratio * ratio)
    u0, u1, u2 = split3(coords)
    t0, t1, t2 = split3(turns)
    g0, g1, g2 = split3(size)
    pad = jnp.zeros((depth - SOURCE_ROWS - 3 * directions, block.shape[1]), jnp.float32)
    none = jnp.zeros((SOURCE_ROWS, block.shape[1]), jnp.float32)
    phase = jnp.concatenate([u0, u0, u1, u0, u2, u1, t0, t1, t2, pad], 0)
    amplitude = jnp.concatenate([none, g0, g1, g2, pad], 0)
    return phase.T.astype(jnp.bfloat16), amplitude.T.astype(jnp.bfloat16)


def source_rows(src, directions, depth):
    s0, s1, s2 = split3(src)
    kinds = lax.broadcasted_iota(jnp.int32, (directions, src.shape[1]), 0).astype(jnp.float32)
    onehot = jnp.where(src[3:4] == kinds, 1.0, 0.0).astype(jnp.bfloat16)
    first = jnp.concatenate([s0, s1], 0).astype(jnp.bfloat16)
    second = jnp.concatenate([s0, s2], 0).astype(jnp.bfloat16)
    pad = jnp.zeros((depth - SOURCE_ROWS - 3 * directions, src.shape[1]), jnp.bfloat16)
    return jnp.concatenate([first, second, first, onehot, onehot, onehot, pad], 0)


def phasor(turns, size):
    r = turns - lax.round(turns, lax.RoundingMethod.TO_NEAREST_EVEN)
    y = r * r
    s = r * (((y + B2) * y + B1) * y + B0)
    q = s * s
    rest = GUARD - q
    c = rest * lax.rsqrt(rest)
    return size * (0.5 * TOP - q), (size * s) * c


def place(mask, size):
    bits = size.bit_length() - 1
    at = 0 * mask
    for order in range(bits):
        at = at | (((mask >> (bits - 1 - order)) & 1) << order)
    return at


def add_sources(chans, directions, depth, so_ref, lhs, total, *work):
    both, sides = work[:2], work[2:]
    shards, _, width = so_ref.shape
    step = math.gcd(width, STEP)
    per = width // step
    half = 2 * chans * TS
    last = shards * per
    ways = math.gcd(last, WAYS)
    sides[-1][...] = jnp.zeros_like(sides[-1])

    def part(t):
        return so_ref[t // per, :, pl.ds(pl.multiple_of(lax.rem(t, per) * step, step), step)]

    def product(t, into):
        made = source_rows(part(t), directions, depth)
        into[...] = jnp.dot(lhs[...], made, preferred_element_type=jnp.float32)

    def phasors(t, both, sides):
        weights = part(t)[4:]
        for side in range(2):
            for c in range(chans):
                at = (side * chans + c) * TS
                turns = both[at : at + TS]
                size = both[half + at : half + at + TS]
                if side == 0:
                    size = size * weights[c : c + 1]
                re, im = phasor(turns, size)
                sides[2 * at : 2 * at + TS] = re.astype(jnp.bfloat16)
                sides[2 * at + TS : 2 * at + 2 * TS] = im.astype(jnp.bfloat16)

    def collect(sides):
        whole = lax.dot_general(
            sides[:half], sides[half:], (((1,), (1,)), ((), ())), preferred_element_type=jnp.float32
        )
        for at in range(0, half, LANES):
            total[at : at + LANES] += whole[at : at + LANES, at : at + LANES]

    product(0, both[0])

    def turn(t, carry):
        for way in range(ways):
            at = t * ways + way
            product(jnp.minimum(at + 1, last - 1), both[(way + 1) % 2])
            phasors(at, both[way % 2], sides[way % 2])
            collect(sides[(way + 1) % 2])
        return carry

    lax.fori_loop(0, last // ways, turn, 0)
    collect(sides[-1])


def first_kernel(chans, directions, depth, row, size, pairs_ref, st0, st1, so_ref, lhs, total, *work):
    total[...] = jnp.zeros_like(total)
    if row is not None:
        me = lax.axis_index("src")
        pair = place(pairs_ref[pl.ds(me * row[0] + row[1], 1)] ^ me, size)
    for side in range(2):
        if row is None:
            block = st0[side]
        else:
            at = jnp.broadcast_to(pair[:, side : side + 1], st0.shape[1:])
            block = jnp.zeros(st0.shape[1:], jnp.float32)
            for n in range(st0.shape[0]):
                block = jnp.where(at == n, st0[n], block)
                block = jnp.where(at == n + st0.shape[0], st1[n], block)
        phase, amplitude = station_rows(block, directions, depth)
        lhs[side * LANES : (side + 1) * LANES] = phase
        lhs[(2 + side) * LANES : (3 + side) * LANES] = amplitude
    add_sources(chans, directions, depth, so_ref, lhs, total, *work)


def next_kernel(chans, directions, depth, lhs, before, so_ref, total, *work):
    total[...] = before[...]
    add_sources(chans, directions, depth, so_ref, lhs, total, *work)


def last_kernel(chans, directions, depth, row, pairs_ref, lhs, before, so_ref, out_ref, total, *work):
    total[...] = before[...]
    add_sources(chans, directions, depth, so_ref, lhs, total, *work)
    me = lax.axis_index("src") * row[0] + row[1]
    pair = pairs_ref[pl.ds(me, 1)]
    same = pair[:, 0:1] == pair[:, 1:2]
    high = lax.broadcasted_iota(jnp.int32, (8, LANES), 0)
    lane = lax.broadcasted_iota(jnp.int32, (8, LANES), 1)
    fold = LANES // TS
    clear = jnp.logical_and(lane % TS == high * fold + lane // TS, same)
    for c in range(chans):
        base = 2 * c * TS
        column = base % LANES
        real = jnp.zeros((8, LANES), jnp.float32)
        imag = jnp.zeros((8, LANES), jnp.float32)
        for b in range(fold):
            w_re = total[pl.ds(base + b, 8, stride=fold)]
            w_im = total[pl.ds(base + TS + b, 8, stride=fold)]
            here = lane // TS == b
            one = (b * TS - column) % LANES
            two = (b * TS - column - TS) % LANES
            real = jnp.where(here, pltpu.roll(w_re, one, 1) + pltpu.roll(w_im, two, 1), real)
            imag = jnp.where(here, pltpu.roll(w_im, one, 1) - pltpu.roll(w_re, two, 1), imag)
        for n, values in enumerate((real, imag)):
            values = jnp.where(clear, 0.0, values)
            for m in range(8):
                out_ref[c, n : n + 1, m * LANES : (m + 1) * LANES] = values[m : m + 1]


class Predictor:
    def __init__(self, chans, directions, width):
        self.chans, self.directions = chans, directions
        self.depth = -(-(SOURCE_ROWS + 3 * directions) // LANES) * LANES
        step = math.gcd(width, STEP)
        self.work = [pltpu.VMEM((4 * chans * TS, step), jnp.float32)] * 2
        self.work += [pltpu.VMEM((4 * chans * TS, step), jnp.bfloat16)] * 2
        self.total = (2 * chans * TS, LANES)

    def call(self, kernel, out_shape, scratch, args):
        vmem = pl.BlockSpec(memory_space=pltpu.VMEM)
        sources = args[-1].shape[0] * args[-1].shape[2]
        count = 2 * self.chans * TS * sources
        return pl.pallas_call(
            kernel,
            out_shape=out_shape,
            in_specs=[vmem] * len(args),
            out_specs=jax.tree.map(lambda _: vmem, out_shape),
            scratch_shapes=scratch,
            compiler_params=pltpu.CompilerParams(vmem_limit_bytes=32 << 20),
            cost_estimate=pl.CostEstimate(flops=2000 * count, bytes_accessed=0, transcendentals=count),
        )(*args)

    def first(self, row, size, pairs, stations, sources):
        kernel = functools.partial(first_kernel, self.chans, self.directions, self.depth, row, size)
        shapes = (
            jax.ShapeDtypeStruct((4 * LANES, self.depth), jnp.bfloat16),
            jax.ShapeDtypeStruct(self.total, jnp.float32),
        )
        return self.call(kernel, shapes, self.work, (pairs, *stations, sources))

    def next(self, lhs, total, sources):
        kernel = functools.partial(next_kernel, self.chans, self.directions, self.depth)
        shape = jax.ShapeDtypeStruct(self.total, jnp.float32)
        return self.call(kernel, shape, self.work, (lhs, total, sources))

    def last(self, row, pairs, lhs, total, sources):
        kernel = functools.partial(last_kernel, self.chans, self.directions, self.depth, row)
        shape = jax.ShapeDtypeStruct((self.chans, 2, TS * TS), jnp.float32)
        scratch = [pltpu.VMEM(self.total, jnp.float32)] + self.work
        return self.call(kernel, shape, scratch, (pairs, lhs, total, sources))


def pack_kernel(scale, chans, channel_ref, positions_ref, flux_ref, cluster_ref, jones_ref, uvw_ref, station_ref, source_ref):
    own = uvw_ref.shape[1]
    directions = jones_ref.shape[2]
    coords = positions_ref[...]
    l_term, m_term = coords[0:1], coords[1:2]
    source_ref[0, 0:2] = coords
    source_ref[0, 2:3] = jnp.sqrt(1.0 - l_term * l_term - m_term * m_term) - 1.0
    source_ref[0, 3:4] = cluster_ref[...].astype(jnp.float32)
    source_ref[0, 4:] = flux_ref[...] * scale
    station_ref[...] = jnp.zeros_like(station_ref)
    for c in range(chans):
        lanes = slice(c * own, (c + 1) * own)
        ratio = 1.0 + 0.002 * channel_ref[c].astype(jnp.float32)
        station_ref[0, 0:3, lanes] = uvw_ref[...] * ratio
        for n in range(2):
            begin = COORD_ROWS + n * directions
            station_ref[0, begin : begin + directions, lanes] = jones_ref[c, n]


def pack(positions, flux, cluster, jones, station_uvw, channels, scale):
    chans, _, directions, own = jones.shape
    vmem = pl.BlockSpec(memory_space=pltpu.VMEM)
    return pl.pallas_call(
        functools.partial(pack_kernel, scale, chans),
        out_shape=(
            jax.ShapeDtypeStruct((1, COORD_ROWS + 2 * directions, chans * own), jnp.float32),
            jax.ShapeDtypeStruct((1, 4 + chans, positions.shape[1]), jnp.float32),
        ),
        in_specs=[pl.BlockSpec(memory_space=pltpu.SMEM)] + [vmem] * 5,
        out_specs=(vmem, vmem),
    )(channels, positions, flux, cluster[None], jones, station_uvw)


def swap(x, bit, size):
    return lax.ppermute(x, "src", [(i, i ^ bit) for i in range(size)])


def after(x, *earlier):
    return lax.optimization_barrier((x, *earlier))[0]


def spread(station, source, size):
    bit = size // 2
    got = None
    while bit:
        arrived = swap(station, bit, size)
        if bit > 1:
            got = swap(source if got is None else after(source, arrived), bit, size)
            station = jnp.concatenate([station, arrived], 0)
        if bit > 2:
            source = jnp.concatenate([source, got], 0)
        bit //= 2
    return (station, arrived), source, got


def on_device(positions, flux, cluster, jones, station_uvw, channels, tile_map):
    size = lax.axis_size("src")
    chans, _, directions, own = jones.shape
    scale = 1.0 / math.sqrt(positions.shape[1] * size)
    station, source = pack(positions, flux, cluster, jones, station_uvw, channels, scale)
    stations, source, got = spread(station, source, size)
    own_rows = tile_map.shape[0] // size
    many = TS // own
    predictor = Predictor(chans, directions, positions.shape[1])
    begun = []
    for row in range(own_rows):
        if many == 1:
            begun.append(predictor.first((own_rows, row), size, tile_map, stations, source))
        else:
            me = lax.axis_index("src")
            pair = lax.dynamic_slice_in_dim(tile_map, me * own_rows + row, 1, 0)[0]
            whole = jnp.concatenate(stations, 0)
            of = place((pair[:, None] * many + jnp.arange(many)[None, :]) ^ me, size)
            picked = jnp.take(whole, of.reshape(-1), axis=0)
            picked = picked.reshape(2, many, whole.shape[1], chans, own)
            picked = jnp.transpose(picked, (0, 2, 3, 1, 4)).reshape(2, whole.shape[1], chans * TS)
            begun.append(predictor.first(None, size, tile_map, (picked, picked), source))
    both = jnp.concatenate([after(source, begun[-1][-1]), got], 0)
    other = swap(both, 1, size)
    out = []
    for row, (lhs, total) in enumerate(begun):
        total = predictor.next(lhs, total, got)
        out.append(predictor.last((own_rows, row), tile_map, lhs, total, other))
    return jnp.stack(out)


def solution(mesh):
    in_specs = (
        P(None, ("group", "src")),
        P(None, ("group", "src")),
        P(("group", "src")),
        P(None, None, None, ("group", "src")),
        P(None, ("group", "src")),
        P("group"),
        P("group", None),
    )
    out_specs = P(("group", "src"), None, None, None)
    return jax.shard_map(
        on_device, mesh=mesh, in_specs=in_specs, out_specs=out_specs, check_vma=False
    )
```

```python
import functools
import math

import jax
import jax.numpy as jnp
from jax import lax
from jax.experimental import pallas as pl
from jax.experimental.pallas import tpu as pltpu
from jax.sharding import PartitionSpec as P

TS = 32
LANES = 128
STEP = 256
WAYS = 16

A0, A1, A2, A3 = 3.1415628696601985, -5.166617869525222, 2.538088675224665, -0.546492984410238
B0, B1, B2 = A0 / A3, A1 / A3, A2 / A3
TOP = 1.0 / (A3 * A3)
GUARD = TOP * (1.0 + 1e-6)
SCALE = 2.0 * A3 * A3

COORD_ROWS = 8
SOURCE_ROWS = 6 * COORD_ROWS


def split3(x):
    a = x.astype(jnp.bfloat16).astype(jnp.float32)
    b = (x - a).astype(jnp.bfloat16).astype(jnp.float32)
    return a, b, x - a - b


def station_rows(block, directions, depth):
    coords = block[:COORD_ROWS]
    re = block[COORD_ROWS : COORD_ROWS + directions]
    im = block[COORD_ROWS + directions :]
    turns = jnp.arctan2(im, re) * (-0.5 / math.pi)
    big = jnp.maximum(jnp.abs(re), jnp.abs(im))
    small = jnp.minimum(jnp.abs(re), jnp.abs(im))
    ratio = small / jnp.where(big == 0.0, 1.0, big)
    size = SCALE * big * jnp.sqrt(1.0 + ratio * ratio)
    u0, u1, u2 = split3(coords)
    t0, t1, t2 = split3(turns)
    g0, g1, g2 = split3(size)
    pad = jnp.zeros((depth - SOURCE_ROWS - 3 * directions, block.shape[1]), jnp.float32)
    none = jnp.zeros((SOURCE_ROWS, block.shape[1]), jnp.float32)
    phase = jnp.concatenate([u0, u0, u1, u0, u2, u1, t0, t1, t2, pad], 0)
    amplitude = jnp.concatenate([none, g0, g1, g2, pad], 0)
    rest = jnp.zeros((LANES - directions, block.shape[1]), jnp.float32)
    return phase.T.astype(jnp.bfloat16), amplitude.T.astype(jnp.bfloat16), jnp.concatenate([size, rest], 0).T


def source_rows(src, directions, depth):
    s0, s1, s2 = split3(src)
    kinds = lax.broadcasted_iota(jnp.int32, (directions, src.shape[1]), 0).astype(jnp.float32)
    onehot = jnp.where(src[3:4] == kinds, 1.0, 0.0).astype(jnp.bfloat16)
    first = jnp.concatenate([s0, s1], 0).astype(jnp.bfloat16)
    second = jnp.concatenate([s0, s2], 0).astype(jnp.bfloat16)
    pad = jnp.zeros((depth - SOURCE_ROWS - 3 * directions, src.shape[1]), jnp.bfloat16)
    return jnp.concatenate([first, second, first, onehot, onehot, onehot, pad], 0)


def phasor(turns, size):
    r = turns - lax.round(turns, lax.RoundingMethod.TO_NEAREST_EVEN)
    y = r * r
    s = r * (((y + B2) * y + B1) * y + B0)
    q = s * s
    rest = GUARD - q
    c = rest * lax.rsqrt(rest)
    return size * (0.5 * TOP - q), (size * s) * c


def steps(size):
    high = [1 << n for n in range(size.bit_length() - 2, 1, -1)]
    return high[:1] + [2] + high[1:] + [1]


def place(mask, size):
    at = 0 * mask
    for order, bit in enumerate(steps(size)):
        at = at | (((mask >> (bit.bit_length() - 1)) & 1) << order)
    return at


def look_up(table, lanes):
    return jnp.take_along_axis(table, lanes, axis=1, mode="promise_in_bounds")


def add_sources(chans, directions, depth, so_ref, lhs, sizes, total, *work):
    both, sides = work[:2], work[2:]
    shards, _, width = so_ref.shape
    step = math.gcd(width, STEP)
    per = width // step
    half = 2 * chans * TS
    last = shards * per
    ways = math.gcd(last, WAYS)
    sides[-1][...] = jnp.zeros_like(sides[-1])

    def part(t):
        return so_ref[t // per, :, pl.ds(pl.multiple_of(lax.rem(t, per) * step, step), step)]

    def product(t, into):
        made = source_rows(part(t), directions, depth)
        into[...] = jnp.dot(lhs[...], made, preferred_element_type=jnp.float32)

    def phasors(t, both, sides):
        src = part(t)
        kinds = jnp.broadcast_to(src[3:4].astype(jnp.int32), (TS, step))
        for side in range(2):
            for c in range(chans):
                at = (side * chans + c) * TS
                turns = both[at : at + TS]
                if side == 0:
                    size = both[half + at : half + at + TS] * src[4 + c : 5 + c]
                else:
                    table = sizes[c * TS : (c + 1) * TS]
                    size = jnp.concatenate([look_up(table, kinds[:, n : n + LANES]) for n in range(0, step, LANES)], 1)
                re, im = phasor(turns, size)
                sides[2 * at : 2 * at + TS] = re.astype(jnp.bfloat16)
                sides[2 * at + TS : 2 * at + 2 * TS] = im.astype(jnp.bfloat16)

    def collect(sides):
        whole = lax.dot_general(
            sides[:half], sides[half:], (((1,), (1,)), ((), ())), preferred_element_type=jnp.float32
        )
        for at in range(0, half, LANES):
            total[at : at + LANES] += whole[at : at + LANES, at : at + LANES]

    product(0, both[0])

    def turn(t, carry):
        for way in range(ways):
            at = t * ways + way
            product(jnp.minimum(at + 1, last - 1), both[(way + 1) % 2])
            phasors(at, both[way % 2], sides[way % 2])
            collect(sides[(way + 1) % 2])
        return carry

    lax.fori_loop(0, last // ways, turn, 0)
    collect(sides[-1])


def first_kernel(chans, directions, depth, row, size, pairs_ref, st0, st1, so_ref, lhs, sizes, total, *work):
    total[...] = jnp.zeros_like(total)
    if row is not None:
        me = lax.axis_index("src")
        pair = place(pairs_ref[pl.ds(me * row[0] + row[1], 1)] ^ me, size)
    for side in range(2):
        if row is None:
            block = st0[side]
        else:
            at = jnp.broadcast_to(pair[:, side : side + 1], st0.shape[1:])
            block = jnp.zeros(st0.shape[1:], jnp.float32)
            for n in range(st0.shape[0]):
                block = jnp.where(at == n, st0[n], block)
                block = jnp.where(at == n + st0.shape[0], st1[n], block)
        phase, amplitude, size = station_rows(block, directions, depth)
        lhs[side * LANES : (side + 1) * LANES] = phase
        if side == 0:
            lhs[2 * LANES : 3 * LANES] = amplitude
        else:
            sizes[...] = size
    add_sources(chans, directions, depth, so_ref, lhs, sizes, total, *work)


def next_kernel(chans, directions, depth, lhs, sizes, before, so_ref, total, *work):
    total[...] = before[...]
    add_sources(chans, directions, depth, so_ref, lhs, sizes, total, *work)


def last_kernel(chans, directions, depth, row, pairs_ref, lhs, sizes, before, so_ref, out_ref, total, *work):
    total[...] = before[...]
    add_sources(chans, directions, depth, so_ref, lhs, sizes, total, *work)
    me = lax.axis_index("src") * row[0] + row[1]
    pair = pairs_ref[pl.ds(me, 1)]
    same = pair[:, 0:1] == pair[:, 1:2]
    high = lax.broadcasted_iota(jnp.int32, (8, LANES), 0)
    lane = lax.broadcasted_iota(jnp.int32, (8, LANES), 1)
    fold = LANES // TS
    clear = jnp.logical_and(lane % TS == high * fold + lane // TS, same)
    for c in range(chans):
        base = 2 * c * TS
        column = base % LANES
        real = jnp.zeros((8, LANES), jnp.float32)
        imag = jnp.zeros((8, LANES), jnp.float32)
        for b in range(fold):
            w_re = total[pl.ds(base + b, 8, stride=fold)]
            w_im = total[pl.ds(base + TS + b, 8, stride=fold)]
            here = lane // TS == b
            one = (b * TS - column) % LANES
            two = (b * TS - column - TS) % LANES
            real = jnp.where(here, pltpu.roll(w_re, one, 1) + pltpu.roll(w_im, two, 1), real)
            imag = jnp.where(here, pltpu.roll(w_im, one, 1) - pltpu.roll(w_re, two, 1), imag)
        for n, values in enumerate((real, imag)):
            values = jnp.where(clear, 0.0, values)
            for m in range(8):
                out_ref[c, n : n + 1, m * LANES : (m + 1) * LANES] = values[m : m + 1]


class Predictor:
    def __init__(self, chans, directions, width):
        self.chans, self.directions = chans, directions
        self.depth = -(-(SOURCE_ROWS + 3 * directions) // LANES) * LANES
        step = math.gcd(width, STEP)
        self.work = [pltpu.VMEM((3 * chans * TS, step), jnp.float32)] * 2
        self.work += [pltpu.VMEM((4 * chans * TS, step), jnp.bfloat16)] * 2
        self.total = (2 * chans * TS, LANES)

    def call(self, kernel, out_shape, scratch, args):
        vmem = pl.BlockSpec(memory_space=pltpu.VMEM)
        sources = args[-1].shape[0] * args[-1].shape[2]
        count = 2 * self.chans * TS * sources
        return pl.pallas_call(
            kernel,
            out_shape=out_shape,
            in_specs=[vmem] * len(args),
            out_specs=jax.tree.map(lambda _: vmem, out_shape),
            scratch_shapes=scratch,
            compiler_params=pltpu.CompilerParams(vmem_limit_bytes=32 << 20),
            cost_estimate=pl.CostEstimate(flops=2000 * count, bytes_accessed=0, transcendentals=count),
        )(*args)

    def first(self, row, size, pairs, stations, sources):
        kernel = functools.partial(first_kernel, self.chans, self.directions, self.depth, row, size)
        shapes = (
            jax.ShapeDtypeStruct((3 * LANES, self.depth), jnp.bfloat16),
            jax.ShapeDtypeStruct((LANES, LANES), jnp.float32),
            jax.ShapeDtypeStruct(self.total, jnp.float32),
        )
        return self.call(kernel, shapes, self.work, (pairs, *stations, sources))

    def next(self, lhs, sizes, total, sources):
        kernel = functools.partial(next_kernel, self.chans, self.directions, self.depth)
        shape = jax.ShapeDtypeStruct(self.total, jnp.float32)
        return self.call(kernel, shape, self.work, (lhs, sizes, total, sources))

    def last(self, row, pairs, lhs, sizes, total, sources):
        kernel = functools.partial(last_kernel, self.chans, self.directions, self.depth, row)
        shape = jax.ShapeDtypeStruct((self.chans, 2, TS * TS), jnp.float32)
        scratch = [pltpu.VMEM(self.total, jnp.float32)] + self.work
        return self.call(kernel, shape, scratch, (pairs, lhs, sizes, total, sources))


def pack_kernel(scale, chans, channel_ref, positions_ref, flux_ref, cluster_ref, jones_ref, uvw_ref, station_ref, source_ref):
    own = uvw_ref.shape[1]
    directions = jones_ref.shape[2]
    coords = positions_ref[...]
    l_term, m_term = coords[0:1], coords[1:2]
    source_ref[0, 0:2] = coords
    source_ref[0, 2:3] = jnp.sqrt(1.0 - l_term * l_term - m_term * m_term) - 1.0
    source_ref[0, 3:4] = cluster_ref[...].astype(jnp.float32)
    source_ref[0, 4:] = flux_ref[...] * scale
    station_ref[...] = jnp.zeros_like(station_ref)
    for c in range(chans):
        lanes = slice(c * own, (c + 1) * own)
        ratio = 1.0 + 0.002 * channel_ref[c].astype(jnp.float32)
        station_ref[0, 0:3, lanes] = uvw_ref[...] * ratio
        for n in range(2):
            begin = COORD_ROWS + n * directions
            station_ref[0, begin : begin + directions, lanes] = jones_ref[c, n]


def pack(positions, flux, cluster, jones, station_uvw, channels, scale):
    chans, _, directions, own = jones.shape
    vmem = pl.BlockSpec(memory_space=pltpu.VMEM)
    return pl.pallas_call(
        functools.partial(pack_kernel, scale, chans),
        out_shape=(
            jax.ShapeDtypeStruct((1, COORD_ROWS + 2 * directions, chans * own), jnp.float32),
            jax.ShapeDtypeStruct((1, 4 + chans, positions.shape[1]), jnp.float32),
        ),
        in_specs=[pl.BlockSpec(memory_space=pltpu.SMEM)] + [vmem] * 5,
        out_specs=(vmem, vmem),
    )(channels, positions, flux, cluster[None], jones, station_uvw)


def swap(x, bit, size):
    return lax.ppermute(x, "src", [(i, i ^ bit) for i in range(size)])


def after(x, *earlier):
    return lax.optimization_barrier((x, *earlier))[0]


def spread(station, source, size):
    arrived = None
    for bit in steps(size):
        ready = source if arrived is None else after(source, arrived)
        arrived = swap(station, bit, size)
        if bit > 2:
            source = jnp.concatenate([source, swap(ready, bit, size)], 0)
        if bit > 1:
            station = jnp.concatenate([station, arrived], 0)
    return (station, arrived), source, swap(after(source, station), 2, size)


def on_device(positions, flux, cluster, jones, station_uvw, channels, tile_map):
    size = lax.axis_size("src")
    chans, _, directions, own = jones.shape
    scale = 1.0 / math.sqrt(positions.shape[1] * size)
    station, source = pack(positions, flux, cluster, jones, station_uvw, channels, scale)
    stations, source, got = spread(station, source, size)
    own_rows = tile_map.shape[0] // size
    many = TS // own
    predictor = Predictor(chans, directions, positions.shape[1])
    begun = []
    for row in range(own_rows):
        if many == 1:
            begun.append(predictor.first((own_rows, row), size, tile_map, stations, source))
        else:
            me = lax.axis_index("src")
            pair = lax.dynamic_slice_in_dim(tile_map, me * own_rows + row, 1, 0)[0]
            whole = jnp.concatenate(stations, 0)
            of = place((pair[:, None] * many + jnp.arange(many)[None, :]) ^ me, size)
            picked = jnp.take(whole, of.reshape(-1), axis=0)
            picked = picked.reshape(2, many, whole.shape[1], chans, own)
            picked = jnp.transpose(picked, (0, 2, 3, 1, 4)).reshape(2, whole.shape[1], chans * TS)
            begun.append(predictor.first(None, size, tile_map, (picked, picked), source))
    both = jnp.concatenate([after(source, begun[-1][-1]), got], 0)
    other = swap(both, 1, size)
    out = []
    for row, (lhs, sizes, total) in enumerate(begun):
        total = predictor.next(lhs, sizes, total, got)
        out.append(predictor.last((own_rows, row), tile_map, lhs, sizes, total, other))
    return jnp.stack(out)


def solution(mesh):
    in_specs = (
        P(None, ("group", "src")),
        P(None, ("group", "src")),
        P(("group", "src")),
        P(None, None, None, ("group", "src")),
        P(None, ("group", "src")),
        P("group"),
        P("group", None),
    )
    out_specs = P(("group", "src"), None, None, None)
    return jax.shard_map(
        on_device, mesh=mesh, in_specs=in_specs, out_specs=out_specs, check_vma=False
    )
```

```python
import functools
import math

import jax
import jax.numpy as jnp
from jax import lax
from jax.experimental import pallas as pl
from jax.experimental.pallas import tpu as pltpu
from jax.sharding import PartitionSpec as P

TS = 32
LANES = 128
STEP = 256
WAYS = 16

A0, A1, A2, A3 = 3.1415628696601985, -5.166617869525222, 2.538088675224665, -0.546492984410238
B0, B1, B2 = A0 / A3, A1 / A3, A2 / A3
TOP = 1.0 / (A3 * A3)
GUARD = TOP * (1.0 + 1e-6)
SCALE = 2.0 * A3 * A3

COORD_ROWS = 8
SOURCE_ROWS = 6 * COORD_ROWS


def split3(x):
    a = x.astype(jnp.bfloat16).astype(jnp.float32)
    b = (x - a).astype(jnp.bfloat16).astype(jnp.float32)
    return a, b, x - a - b


def station_rows(block, directions, depth):
    coords = block[:COORD_ROWS]
    re = block[COORD_ROWS : COORD_ROWS + directions]
    im = block[COORD_ROWS + directions :]
    turns = jnp.arctan2(im, re) * (-0.5 / math.pi)
    big = jnp.maximum(jnp.abs(re), jnp.abs(im))
    small = jnp.minimum(jnp.abs(re), jnp.abs(im))
    ratio = small / jnp.where(big == 0.0, 1.0, big)
    size = SCALE * big * jnp.sqrt(1.0 + ratio * ratio)
    u0, u1, u2 = split3(coords)
    t0, t1, t2 = split3(turns)
    g0, g1, g2 = split3(size)
    pad = jnp.zeros((depth - SOURCE_ROWS - 3 * directions, block.shape[1]), jnp.float32)
    none = jnp.zeros((SOURCE_ROWS, block.shape[1]), jnp.float32)
    phase = jnp.concatenate([u0, u0, u1, u0, u2, u1, t0, t1, t2, pad], 0)
    amplitude = jnp.concatenate([none, g0, g1, g2, pad], 0)
    rest = jnp.zeros((LANES - directions, block.shape[1]), jnp.float32)
    return phase.T.astype(jnp.bfloat16), amplitude.T.astype(jnp.bfloat16), jnp.concatenate([size, rest], 0).T


def source_rows(src, directions, depth):
    s0, s1, s2 = split3(src)
    kinds = lax.broadcasted_iota(jnp.int32, (directions, src.shape[1]), 0).astype(jnp.float32)
    onehot = jnp.where(src[3:4] == kinds, 1.0, 0.0).astype(jnp.bfloat16)
    first = jnp.concatenate([s0, s1], 0).astype(jnp.bfloat16)
    second = jnp.concatenate([s0, s2], 0).astype(jnp.bfloat16)
    pad = jnp.zeros((depth - SOURCE_ROWS - 3 * directions, src.shape[1]), jnp.bfloat16)
    return jnp.concatenate([first, second, first, onehot, onehot, onehot, pad], 0)


def phasor(turns, size):
    r = turns - lax.round(turns, lax.RoundingMethod.TO_NEAREST_EVEN)
    y = r * r
    s = r * (((y + B2) * y + B1) * y + B0)
    q = s * s
    rest = GUARD - q
    c = rest * lax.rsqrt(rest)
    return size * (0.5 * TOP - q), (size * s) * c


def steps(size):
    high = [1 << n for n in range(size.bit_length() - 2, 1, -1)]
    return high[:1] + [2] + high[1:] + [1]


def place(mask, size):
    at = 0 * mask
    for order, bit in enumerate(steps(size)):
        at = at | (((mask >> (bit.bit_length() - 1)) & 1) << order)
    return at


def look_up(table, lanes):
    return jnp.take_along_axis(table, lanes, axis=1, mode="promise_in_bounds")


def add_sources(chans, directions, depth, so_ref, lhs, sizes, total, *work):
    both, sides = work[:2], work[2:]
    shards = so_ref.shape[0]
    tiles = so_ref.shape[1] // COORD_ROWS
    wide = math.gcd(tiles, STEP // LANES)
    step = wide * LANES
    per = tiles // wide
    half = 2 * chans * TS
    last = shards * per
    ways = math.gcd(last, WAYS)
    sides[-1][...] = jnp.zeros_like(sides[-1])

    def part(t):
        row = lax.rem(t, per) * (wide * COORD_ROWS)
        rows = [pl.ds(pl.multiple_of(row + n * COORD_ROWS, COORD_ROWS), COORD_ROWS) for n in range(wide)]
        return jnp.concatenate([so_ref[t // per, at] for at in rows], 1)

    def product(t, into):
        made = source_rows(part(t), directions, depth)
        into[...] = jnp.dot(lhs[...], made, preferred_element_type=jnp.float32)

    def phasors(t, both, sides):
        src = part(t)
        kinds = jnp.broadcast_to(src[3:4].astype(jnp.int32), (TS, step))
        for side in range(2):
            for c in range(chans):
                at = (side * chans + c) * TS
                turns = both[at : at + TS]
                if side == 0:
                    size = both[half + at : half + at + TS] * src[4 + c : 5 + c]
                else:
                    table = sizes[c * TS : (c + 1) * TS]
                    size = jnp.concatenate([look_up(table, kinds[:, n : n + LANES]) for n in range(0, step, LANES)], 1)
                re, im = phasor(turns, size)
                sides[2 * at : 2 * at + TS] = re.astype(jnp.bfloat16)
                sides[2 * at + TS : 2 * at + 2 * TS] = im.astype(jnp.bfloat16)

    def collect(sides):
        whole = lax.dot_general(
            sides[:half], sides[half:], (((1,), (1,)), ((), ())), preferred_element_type=jnp.float32
        )
        for at in range(0, half, LANES):
            total[at : at + LANES] += whole[at : at + LANES, at : at + LANES]

    product(0, both[0])

    def turn(t, carry):
        for way in range(ways):
            at = t * ways + way
            product(jnp.minimum(at + 1, last - 1), both[(way + 1) % 2])
            phasors(at, both[way % 2], sides[way % 2])
            collect(sides[(way + 1) % 2])
        return carry

    lax.fori_loop(0, last // ways, turn, 0)
    collect(sides[-1])


def first_kernel(chans, directions, depth, row, size, pairs_ref, st0, st1, so_ref, lhs, sizes, total, *work):
    total[...] = jnp.zeros_like(total)
    if row is not None:
        me = lax.axis_index("src")
        pair = place(pairs_ref[pl.ds(me * row[0] + row[1], 1)] ^ me, size)
    for side in range(2):
        if row is None:
            block = st0[side]
        else:
            at = jnp.broadcast_to(pair[:, side : side + 1], st0.shape[1:])
            block = jnp.zeros(st0.shape[1:], jnp.float32)
            for n in range(st0.shape[0]):
                block = jnp.where(at == n, st0[n], block)
                block = jnp.where(at == n + st0.shape[0], st1[n], block)
        phase, amplitude, size = station_rows(block, directions, depth)
        lhs[side * LANES : (side + 1) * LANES] = phase
        if side == 0:
            lhs[2 * LANES : 3 * LANES] = amplitude
        else:
            sizes[...] = size
    add_sources(chans, directions, depth, so_ref, lhs, sizes, total, *work)


def next_kernel(chans, directions, depth, lhs, sizes, before, so_ref, total, *work):
    total[...] = before[...]
    add_sources(chans, directions, depth, so_ref, lhs, sizes, total, *work)


def last_kernel(chans, directions, depth, row, pairs_ref, lhs, sizes, before, so_ref, out_ref, total, *work):
    total[...] = before[...]
    add_sources(chans, directions, depth, so_ref, lhs, sizes, total, *work)
    me = lax.axis_index("src") * row[0] + row[1]
    pair = pairs_ref[pl.ds(me, 1)]
    same = pair[:, 0:1] == pair[:, 1:2]
    high = lax.broadcasted_iota(jnp.int32, (8, LANES), 0)
    lane = lax.broadcasted_iota(jnp.int32, (8, LANES), 1)
    fold = LANES // TS
    clear = jnp.logical_and(lane % TS == high * fold + lane // TS, same)
    for c in range(chans):
        base = 2 * c * TS
        column = base % LANES
        real = jnp.zeros((8, LANES), jnp.float32)
        imag = jnp.zeros((8, LANES), jnp.float32)
        for b in range(fold):
            w_re = total[pl.ds(base + b, 8, stride=fold)]
            w_im = total[pl.ds(base + TS + b, 8, stride=fold)]
            here = lane // TS == b
            one = (b * TS - column) % LANES
            two = (b * TS - column - TS) % LANES
            real = jnp.where(here, pltpu.roll(w_re, one, 1) + pltpu.roll(w_im, two, 1), real)
            imag = jnp.where(here, pltpu.roll(w_im, one, 1) - pltpu.roll(w_re, two, 1), imag)
        for n, values in enumerate((real, imag)):
            values = jnp.where(clear, 0.0, values)
            for m in range(8):
                out_ref[c, n : n + 1, m * LANES : (m + 1) * LANES] = values[m : m + 1]


class Predictor:
    def __init__(self, chans, directions, width):
        self.chans, self.directions = chans, directions
        self.depth = -(-(SOURCE_ROWS + 3 * directions) // LANES) * LANES
        step = math.gcd(width, STEP)
        self.work = [pltpu.VMEM((3 * chans * TS, step), jnp.float32)] * 2
        self.work += [pltpu.VMEM((4 * chans * TS, step), jnp.bfloat16)] * 2
        self.total = (2 * chans * TS, LANES)

    def call(self, kernel, out_shape, scratch, args):
        vmem = pl.BlockSpec(memory_space=pltpu.VMEM)
        sources = args[-1].size // COORD_ROWS
        count = 2 * self.chans * TS * sources
        return pl.pallas_call(
            kernel,
            out_shape=out_shape,
            in_specs=[vmem] * len(args),
            out_specs=jax.tree.map(lambda _: vmem, out_shape),
            scratch_shapes=scratch,
            compiler_params=pltpu.CompilerParams(vmem_limit_bytes=32 << 20),
            cost_estimate=pl.CostEstimate(flops=2000 * count, bytes_accessed=0, transcendentals=count),
        )(*args)

    def first(self, row, size, pairs, stations, sources):
        kernel = functools.partial(first_kernel, self.chans, self.directions, self.depth, row, size)
        shapes = (
            jax.ShapeDtypeStruct((3 * LANES, self.depth), jnp.bfloat16),
            jax.ShapeDtypeStruct((LANES, LANES), jnp.float32),
            jax.ShapeDtypeStruct(self.total, jnp.float32),
        )
        return self.call(kernel, shapes, self.work, (pairs, *stations, sources))

    def next(self, lhs, sizes, total, sources):
        kernel = functools.partial(next_kernel, self.chans, self.directions, self.depth)
        shape = jax.ShapeDtypeStruct(self.total, jnp.float32)
        return self.call(kernel, shape, self.work, (lhs, sizes, total, sources))

    def last(self, row, pairs, lhs, sizes, total, sources):
        kernel = functools.partial(last_kernel, self.chans, self.directions, self.depth, row)
        shape = jax.ShapeDtypeStruct((self.chans, 2, TS * TS), jnp.float32)
        scratch = [pltpu.VMEM(self.total, jnp.float32)] + self.work
        return self.call(kernel, shape, scratch, (pairs, lhs, sizes, total, sources))


def pack_kernel(scale, chans, channel_ref, positions_ref, flux_ref, cluster_ref, jones_ref, uvw_ref, station_ref, source_ref):
    own = uvw_ref.shape[1]
    directions = jones_ref.shape[2]
    coords = positions_ref[...]
    l_term, m_term = coords[0:1], coords[1:2]
    n_term = jnp.sqrt(1.0 - l_term * l_term - m_term * m_term) - 1.0
    kinds = cluster_ref[...].astype(jnp.float32)
    source = jnp.concatenate([coords, n_term, kinds, flux_ref[...] * scale], 0)
    for n in range(coords.shape[1] // LANES):
        source_ref[0, n * COORD_ROWS : (n + 1) * COORD_ROWS] = source[:, n * LANES : (n + 1) * LANES]
    station_ref[...] = jnp.zeros_like(station_ref)
    for c in range(chans):
        lanes = slice(c * own, (c + 1) * own)
        ratio = 1.0 + 0.002 * channel_ref[c].astype(jnp.float32)
        station_ref[0, 0:3, lanes] = uvw_ref[...] * ratio
        for n in range(2):
            begin = COORD_ROWS + n * directions
            station_ref[0, begin : begin + directions, lanes] = jones_ref[c, n]


def pack(positions, flux, cluster, jones, station_uvw, channels, scale):
    chans, _, directions, own = jones.shape
    vmem = pl.BlockSpec(memory_space=pltpu.VMEM)
    return pl.pallas_call(
        functools.partial(pack_kernel, scale, chans),
        out_shape=(
            jax.ShapeDtypeStruct((1, COORD_ROWS + 2 * directions, chans * own), jnp.float32),
            jax.ShapeDtypeStruct((1, positions.shape[1] // LANES * COORD_ROWS, LANES), jnp.float32),
        ),
        in_specs=[pl.BlockSpec(memory_space=pltpu.SMEM)] + [vmem] * 5,
        out_specs=(vmem, vmem),
    )(channels, positions, flux, cluster[None], jones, station_uvw)


def swap(x, bit, size):
    return lax.ppermute(x, "src", [(i, i ^ bit) for i in range(size)])


def after(x, *earlier):
    return lax.optimization_barrier((x, *earlier))[0]


def spread(station, source, size):
    arrived = None
    for bit in steps(size):
        ready = source if arrived is None else after(source, arrived)
        arrived = swap(station, bit, size)
        if bit > 2:
            source = jnp.concatenate([source, swap(ready, bit, size)], 0)
        if bit > 1:
            station = jnp.concatenate([station, arrived], 0)
    return (station, arrived), source, swap(after(source, station), 2, size)


def on_device(positions, flux, cluster, jones, station_uvw, channels, tile_map):
    size = lax.axis_size("src")
    chans, _, directions, own = jones.shape
    scale = 1.0 / math.sqrt(positions.shape[1] * size)
    station, source = pack(positions, flux, cluster, jones, station_uvw, channels, scale)
    stations, source, got = spread(station, source, size)
    own_rows = tile_map.shape[0] // size
    many = TS // own
    predictor = Predictor(chans, directions, positions.shape[1])
    begun = []
    for row in range(own_rows):
        if many == 1:
            begun.append(predictor.first((own_rows, row), size, tile_map, stations, source))
        else:
            me = lax.axis_index("src")
            pair = lax.dynamic_slice_in_dim(tile_map, me * own_rows + row, 1, 0)[0]
            whole = jnp.concatenate(stations, 0)
            of = place((pair[:, None] * many + jnp.arange(many)[None, :]) ^ me, size)
            picked = jnp.take(whole, of.reshape(-1), axis=0)
            picked = picked.reshape(2, many, whole.shape[1], chans, own)
            picked = jnp.transpose(picked, (0, 2, 3, 1, 4)).reshape(2, whole.shape[1], chans * TS)
            begun.append(predictor.first(None, size, tile_map, (picked, picked), source))
    both = jnp.concatenate([after(source, begun[-1][-1]), got], 0)
    other = swap(both, 1, size)
    out = []
    for row, (lhs, sizes, total) in enumerate(begun):
        total = predictor.next(lhs, sizes, total, got)
        out.append(predictor.last((own_rows, row), tile_map, lhs, sizes, total, other))
    return jnp.stack(out)


def solution(mesh):
    in_specs = (
        P(None, ("group", "src")),
        P(None, ("group", "src")),
        P(("group", "src")),
        P(None, None, None, ("group", "src")),
        P(None, ("group", "src")),
        P("group"),
        P("group", None),
    )
    out_specs = P(("group", "src"), None, None, None)
    return jax.shard_map(
        on_device, mesh=mesh, in_specs=in_specs, out_specs=out_specs, check_vma=False
    )
```

```python
import functools
import math

import jax
import jax.numpy as jnp
from jax import lax
from jax.experimental import pallas as pl
from jax.experimental.pallas import tpu as pltpu
from jax.sharding import PartitionSpec as P

TS = 32
LANES = 128
STEP = 256
WAYS = 16

A0, A1, A2, A3 = 3.1415628696601985, -5.166617869525222, 2.538088675224665, -0.546492984410238
B0, B1, B2 = A0 / A3, A1 / A3, A2 / A3
TOP = 1.0 / (A3 * A3)
GUARD = TOP * (1.0 + 1e-6)
SCALE = 2.0 * A3 * A3

COORD_ROWS = 8
SOURCE_ROWS = 6 * COORD_ROWS


def split3(x):
    a = x.astype(jnp.bfloat16).astype(jnp.float32)
    b = (x - a).astype(jnp.bfloat16).astype(jnp.float32)
    return a, b, x - a - b


def station_rows(block, directions, depth):
    coords = block[:COORD_ROWS]
    re = block[COORD_ROWS : COORD_ROWS + directions]
    im = block[COORD_ROWS + directions :]
    turns = jnp.arctan2(im, re) * (-0.5 / math.pi)
    big = jnp.maximum(jnp.abs(re), jnp.abs(im))
    small = jnp.minimum(jnp.abs(re), jnp.abs(im))
    ratio = small / jnp.where(big == 0.0, 1.0, big)
    size = SCALE * big * jnp.sqrt(1.0 + ratio * ratio)
    u0, u1, u2 = split3(coords)
    t0, t1, t2 = split3(turns)
    g0, g1, g2 = split3(size)
    pad = jnp.zeros((depth - SOURCE_ROWS - 3 * directions, block.shape[1]), jnp.float32)
    none = jnp.zeros((SOURCE_ROWS, block.shape[1]), jnp.float32)
    phase = jnp.concatenate([u0, u0, u1, u0, u2, u1, t0, t1, t2, pad], 0)
    amplitude = jnp.concatenate([none, g0, g1, g2, pad], 0)
    rest = jnp.zeros((LANES - directions, block.shape[1]), jnp.float32)
    return phase.T.astype(jnp.bfloat16), amplitude.T.astype(jnp.bfloat16), jnp.concatenate([size, rest], 0).T


def source_rows(src, directions, depth):
    s0, s1, s2 = split3(src)
    kinds = lax.broadcasted_iota(jnp.int32, (directions, src.shape[1]), 0).astype(jnp.float32)
    onehot = jnp.where(src[3:4] == kinds, 1.0, 0.0).astype(jnp.bfloat16)
    first = jnp.concatenate([s0, s1], 0).astype(jnp.bfloat16)
    second = jnp.concatenate([s0, s2], 0).astype(jnp.bfloat16)
    pad = jnp.zeros((depth - SOURCE_ROWS - 3 * directions, src.shape[1]), jnp.bfloat16)
    return jnp.concatenate([first, second, first, onehot, onehot, onehot, pad], 0)


def phasor(turns, size):
    r = turns - lax.round(turns, lax.RoundingMethod.TO_NEAREST_EVEN)
    y = r * r
    s = r * (((y + B2) * y + B1) * y + B0)
    q = s * s
    rest = GUARD - q
    c = rest * lax.rsqrt(rest)
    return size * (0.5 * TOP - q), (size * s) * c


def place(mask, size):
    bits = size.bit_length() - 1
    at = 0 * mask
    for order in range(bits):
        at = at | (((mask >> (bits - 1 - order)) & 1) << order)
    return at


def look_up(table, lanes):
    return jnp.take_along_axis(table, lanes, axis=1, mode="promise_in_bounds")


def add_sources(chans, directions, depth, so_ref, lhs, sizes, total, *work):
    both, sides = work[:2], work[2:]
    shards = so_ref.shape[0]
    tiles = so_ref.shape[1] // COORD_ROWS
    wide = math.gcd(tiles, STEP // LANES)
    step = wide * LANES
    per = tiles // wide
    half = 2 * chans * TS
    last = shards * per
    ways = math.gcd(last, WAYS)
    sides[-1][...] = jnp.zeros_like(sides[-1])

    def part(t):
        row = lax.rem(t, per) * (wide * COORD_ROWS)
        rows = [pl.ds(pl.multiple_of(row + n * COORD_ROWS, COORD_ROWS), COORD_ROWS) for n in range(wide)]
        return jnp.concatenate([so_ref[t // per, at] for at in rows], 1)

    def product(t, into):
        made = source_rows(part(t), directions, depth)
        into[...] = jnp.dot(lhs[...], made, preferred_element_type=jnp.float32)

    def phasors(t, both, sides):
        src = part(t)
        kinds = jnp.broadcast_to(src[3:4].astype(jnp.int32), (TS, step))
        for side in range(2):
            for c in range(chans):
                at = (side * chans + c) * TS
                turns = both[at : at + TS]
                if side == 0:
                    size = both[half + at : half + at + TS] * src[4 + c : 5 + c]
                else:
                    table = sizes[c * TS : (c + 1) * TS]
                    size = jnp.concatenate([look_up(table, kinds[:, n : n + LANES]) for n in range(0, step, LANES)], 1)
                re, im = phasor(turns, size)
                sides[2 * at : 2 * at + TS] = re.astype(jnp.bfloat16)
                sides[2 * at + TS : 2 * at + 2 * TS] = im.astype(jnp.bfloat16)

    def collect(sides):
        whole = lax.dot_general(
            sides[:half], sides[half:], (((1,), (1,)), ((), ())), preferred_element_type=jnp.float32
        )
        for at in range(0, half, LANES):
            total[at : at + LANES] += whole[at : at + LANES, at : at + LANES]

    product(0, both[0])

    def turn(t, carry):
        for way in range(ways):
            at = t * ways + way
            product(jnp.minimum(at + 1, last - 1), both[(way + 1) % 2])
            phasors(at, both[way % 2], sides[way % 2])
            collect(sides[(way + 1) % 2])
        return carry

    lax.fori_loop(0, last // ways, turn, 0)
    collect(sides[-1])


def first_kernel(chans, directions, depth, row, size, pairs_ref, st0, st1, so_ref, lhs, sizes, total, *work):
    total[...] = jnp.zeros_like(total)
    if row is not None:
        me = lax.axis_index("src")
        pair = place(pairs_ref[pl.ds(me * row[0] + row[1], 1)] ^ me, size)
    for side in range(2):
        if row is None:
            block = st0[side]
        else:
            at = jnp.broadcast_to(pair[:, side : side + 1], st0.shape[1:])
            block = jnp.zeros(st0.shape[1:], jnp.float32)
            for n in range(st0.shape[0]):
                block = jnp.where(at == n, st0[n], block)
                block = jnp.where(at == n + st0.shape[0], st1[n], block)
        phase, amplitude, size = station_rows(block, directions, depth)
        lhs[side * LANES : (side + 1) * LANES] = phase
        if side == 0:
            lhs[2 * LANES : 3 * LANES] = amplitude
        else:
            sizes[...] = size
    add_sources(chans, directions, depth, so_ref, lhs, sizes, total, *work)


def next_kernel(chans, directions, depth, lhs, sizes, before, so_ref, total, *work):
    total[...] = before[...]
    add_sources(chans, directions, depth, so_ref, lhs, sizes, total, *work)


def last_kernel(chans, directions, depth, row, pairs_ref, lhs, sizes, before, so_ref, out_ref, total, *work):
    total[...] = before[...]
    add_sources(chans, directions, depth, so_ref, lhs, sizes, total, *work)
    me = lax.axis_index("src") * row[0] + row[1]
    pair = pairs_ref[pl.ds(me, 1)]
    same = pair[:, 0:1] == pair[:, 1:2]
    high = lax.broadcasted_iota(jnp.int32, (8, LANES), 0)
    lane = lax.broadcasted_iota(jnp.int32, (8, LANES), 1)
    fold = LANES // TS
    clear = jnp.logical_and(lane % TS == high * fold + lane // TS, same)
    for c in range(chans):
        base = 2 * c * TS
        column = base % LANES
        real = jnp.zeros((8, LANES), jnp.float32)
        imag = jnp.zeros((8, LANES), jnp.float32)
        for b in range(fold):
            w_re = total[pl.ds(base + b, 8, stride=fold)]
            w_im = total[pl.ds(base + TS + b, 8, stride=fold)]
            here = lane // TS == b
            one = (b * TS - column) % LANES
            two = (b * TS - column - TS) % LANES
            real = jnp.where(here, pltpu.roll(w_re, one, 1) + pltpu.roll(w_im, two, 1), real)
            imag = jnp.where(here, pltpu.roll(w_im, one, 1) - pltpu.roll(w_re, two, 1), imag)
        for n, values in enumerate((real, imag)):
            values = jnp.where(clear, 0.0, values)
            for m in range(8):
                out_ref[c, n : n + 1, m * LANES : (m + 1) * LANES] = values[m : m + 1]


class Predictor:
    def __init__(self, chans, directions, width):
        self.chans, self.directions = chans, directions
        self.depth = -(-(SOURCE_ROWS + 3 * directions) // LANES) * LANES
        step = math.gcd(width, STEP)
        self.work = [pltpu.VMEM((3 * chans * TS, step), jnp.float32)] * 2
        self.work += [pltpu.VMEM((4 * chans * TS, step), jnp.bfloat16)] * 2
        self.total = (2 * chans * TS, LANES)

    def call(self, kernel, out_shape, scratch, args):
        vmem = pl.BlockSpec(memory_space=pltpu.VMEM)
        sources = args[-1].size // COORD_ROWS
        count = 2 * self.chans * TS * sources
        return pl.pallas_call(
            kernel,
            out_shape=out_shape,
            in_specs=[vmem] * len(args),
            out_specs=jax.tree.map(lambda _: vmem, out_shape),
            scratch_shapes=scratch,
            compiler_params=pltpu.CompilerParams(vmem_limit_bytes=32 << 20),
            cost_estimate=pl.CostEstimate(flops=2000 * count, bytes_accessed=0, transcendentals=count),
        )(*args)

    def first(self, row, size, pairs, stations, sources):
        kernel = functools.partial(first_kernel, self.chans, self.directions, self.depth, row, size)
        shapes = (
            jax.ShapeDtypeStruct((3 * LANES, self.depth), jnp.bfloat16),
            jax.ShapeDtypeStruct((LANES, LANES), jnp.float32),
            jax.ShapeDtypeStruct(self.total, jnp.float32),
        )
        return self.call(kernel, shapes, self.work, (pairs, *stations, sources))

    def next(self, lhs, sizes, total, sources):
        kernel = functools.partial(next_kernel, self.chans, self.directions, self.depth)
        shape = jax.ShapeDtypeStruct(self.total, jnp.float32)
        return self.call(kernel, shape, self.work, (lhs, sizes, total, sources))

    def last(self, row, pairs, lhs, sizes, total, sources):
        kernel = functools.partial(last_kernel, self.chans, self.directions, self.depth, row)
        shape = jax.ShapeDtypeStruct((self.chans, 2, TS * TS), jnp.float32)
        scratch = [pltpu.VMEM(self.total, jnp.float32)] + self.work
        return self.call(kernel, shape, scratch, (pairs, lhs, sizes, total, sources))


def pack_kernel(scale, chans, channel_ref, positions_ref, flux_ref, cluster_ref, jones_ref, uvw_ref, station_ref, source_ref):
    own = uvw_ref.shape[1]
    directions = jones_ref.shape[2]
    coords = positions_ref[...]
    l_term, m_term = coords[0:1], coords[1:2]
    n_term = jnp.sqrt(1.0 - l_term * l_term - m_term * m_term) - 1.0
    kinds = cluster_ref[...].astype(jnp.float32)
    source = jnp.concatenate([coords, n_term, kinds, flux_ref[...] * scale], 0)
    for n in range(coords.shape[1] // LANES):
        source_ref[0, n * COORD_ROWS : (n + 1) * COORD_ROWS] = source[:, n * LANES : (n + 1) * LANES]
    station_ref[...] = jnp.zeros_like(station_ref)
    for c in range(chans):
        lanes = slice(c * own, (c + 1) * own)
        ratio = 1.0 + 0.002 * channel_ref[c].astype(jnp.float32)
        station_ref[0, 0:3, lanes] = uvw_ref[...] * ratio
        for n in range(2):
            begin = COORD_ROWS + n * directions
            station_ref[0, begin : begin + directions, lanes] = jones_ref[c, n]


def pack(positions, flux, cluster, jones, station_uvw, channels, scale):
    chans, _, directions, own = jones.shape
    vmem = pl.BlockSpec(memory_space=pltpu.VMEM)
    return pl.pallas_call(
        functools.partial(pack_kernel, scale, chans),
        out_shape=(
            jax.ShapeDtypeStruct((1, COORD_ROWS + 2 * directions, chans * own), jnp.float32),
            jax.ShapeDtypeStruct((1, positions.shape[1] // LANES * COORD_ROWS, LANES), jnp.float32),
        ),
        in_specs=[pl.BlockSpec(memory_space=pltpu.SMEM)] + [vmem] * 5,
        out_specs=(vmem, vmem),
    )(channels, positions, flux, cluster[None], jones, station_uvw)


def swap(x, bit, size):
    return lax.ppermute(x, "src", [(i, i ^ bit) for i in range(size)])


def after(x, *earlier):
    return lax.optimization_barrier((x, *earlier))[0]


def spread(station, source, size):
    bit, arrived = size // 2, None
    while bit > 4:
        ready = source if arrived is None else after(source, arrived)
        arrived = swap(station, bit, size)
        source = jnp.concatenate([source, swap(ready, bit, size)], 0)
        station = jnp.concatenate([station, arrived], 0)
        bit //= 2
    arrived = swap(station, 4, size)
    station = jnp.concatenate([station, arrived], 0)
    ready = after(source, arrived)
    station = jnp.concatenate([station, swap(station, 2, size)], 0)
    across = swap(ready, 2, size)
    other = swap(ready, 4, size)
    across = jnp.concatenate([across, swap(other, 2, size)], 0)
    return (station, swap(station, 1, size)), jnp.concatenate([source, other], 0), across


def on_device(positions, flux, cluster, jones, station_uvw, channels, tile_map):
    size = lax.axis_size("src")
    chans, _, directions, own = jones.shape
    scale = 1.0 / math.sqrt(positions.shape[1] * size)
    station, source = pack(positions, flux, cluster, jones, station_uvw, channels, scale)
    stations, source, got = spread(station, source, size)
    own_rows = tile_map.shape[0] // size
    many = TS // own
    predictor = Predictor(chans, directions, positions.shape[1])
    begun = []
    for row in range(own_rows):
        if many == 1:
            begun.append(predictor.first((own_rows, row), size, tile_map, stations, source))
        else:
            me = lax.axis_index("src")
            pair = lax.dynamic_slice_in_dim(tile_map, me * own_rows + row, 1, 0)[0]
            whole = jnp.concatenate(stations, 0)
            of = place((pair[:, None] * many + jnp.arange(many)[None, :]) ^ me, size)
            picked = jnp.take(whole, of.reshape(-1), axis=0)
            picked = picked.reshape(2, many, whole.shape[1], chans, own)
            picked = jnp.transpose(picked, (0, 2, 3, 1, 4)).reshape(2, whole.shape[1], chans * TS)
            begun.append(predictor.first(None, size, tile_map, (picked, picked), source))
    both = jnp.concatenate([after(source, begun[-1][-1]), got], 0)
    other = swap(both, 1, size)
    out = []
    for row, (lhs, sizes, total) in enumerate(begun):
        total = predictor.next(lhs, sizes, total, got)
        out.append(predictor.last((own_rows, row), tile_map, lhs, sizes, total, other))
    return jnp.stack(out)


def solution(mesh):
    in_specs = (
        P(None, ("group", "src")),
        P(None, ("group", "src")),
        P(("group", "src")),
        P(None, None, None, ("group", "src")),
        P(None, ("group", "src")),
        P("group"),
        P("group", None),
    )
    out_specs = P(("group", "src"), None, None, None)
    return jax.shard_map(
        on_device, mesh=mesh, in_specs=in_specs, out_specs=out_specs, check_vma=False
    )
```

```python
import functools
import math

import jax
import jax.numpy as jnp
from jax import lax
from jax.experimental import pallas as pl
from jax.experimental.pallas import tpu as pltpu
from jax.sharding import PartitionSpec as P

TS = 32
LANES = 128
STEP = 256
WAYS = 16

A0, A1, A2, A3 = 3.1415628696601985, -5.166617869525222, 2.538088675224665, -0.546492984410238
B0, B1, B2 = A0 / A3, A1 / A3, A2 / A3
TOP = 1.0 / (A3 * A3)
GUARD = TOP * (1.0 + 1e-6)
SCALE = 2.0 * A3 * A3

COORD_ROWS = 8
SOURCE_ROWS = 6 * COORD_ROWS


def split3(x):
    a = x.astype(jnp.bfloat16).astype(jnp.float32)
    b = (x - a).astype(jnp.bfloat16).astype(jnp.float32)
    return a, b, x - a - b


def station_rows(block, directions, depth):
    coords = block[:COORD_ROWS]
    re = block[COORD_ROWS : COORD_ROWS + directions]
    im = block[COORD_ROWS + directions :]
    turns = jnp.arctan2(im, re) * (-0.5 / math.pi)
    big = jnp.maximum(jnp.abs(re), jnp.abs(im))
    small = jnp.minimum(jnp.abs(re), jnp.abs(im))
    ratio = small / jnp.where(big == 0.0, 1.0, big)
    size = SCALE * big * jnp.sqrt(1.0 + ratio * ratio)
    u0, u1, u2 = split3(coords)
    t0, t1, t2 = split3(turns)
    g0, g1, g2 = split3(size)
    pad = jnp.zeros((depth - SOURCE_ROWS - 3 * directions, block.shape[1]), jnp.float32)
    none = jnp.zeros((SOURCE_ROWS, block.shape[1]), jnp.float32)
    phase = jnp.concatenate([u0, u0, u1, u0, u2, u1, t0, t1, t2, pad], 0)
    amplitude = jnp.concatenate([none, g0, g1, g2, pad], 0)
    rest = jnp.zeros((LANES - directions, block.shape[1]), jnp.float32)
    return phase.T.astype(jnp.bfloat16), amplitude.T.astype(jnp.bfloat16), jnp.concatenate([size, rest], 0).T


def source_rows(src, directions, depth):
    s0, s1, s2 = split3(src)
    kinds = lax.broadcasted_iota(jnp.int32, (directions, src.shape[1]), 0).astype(jnp.float32)
    onehot = jnp.where(src[3:4] == kinds, 1.0, 0.0).astype(jnp.bfloat16)
    first = jnp.concatenate([s0, s1], 0).astype(jnp.bfloat16)
    second = jnp.concatenate([s0, s2], 0).astype(jnp.bfloat16)
    pad = jnp.zeros((depth - SOURCE_ROWS - 3 * directions, src.shape[1]), jnp.bfloat16)
    return jnp.concatenate([first, second, first, onehot, onehot, onehot, pad], 0)


def phasor(turns, size):
    r = turns - lax.round(turns, lax.RoundingMethod.TO_NEAREST_EVEN)
    y = r * r
    s = r * (((y + B2) * y + B1) * y + B0)
    q = s * s
    rest = GUARD - q
    c = rest * lax.rsqrt(rest)
    return size * (0.5 * TOP - q), (size * s) * c


def place(mask, size):
    bits = size.bit_length() - 1
    at = 0 * mask
    for order in range(bits):
        at = at | (((mask >> (bits - 1 - order)) & 1) << order)
    return at


def look_up(table, lanes):
    return jnp.take_along_axis(table, lanes, axis=1, mode="promise_in_bounds")


def add_sources(chans, directions, depth, so_ref, lhs, sizes, total, *work):
    both, sides = work[:2], work[2:]
    shards = so_ref.shape[0]
    tiles = so_ref.shape[1] // COORD_ROWS
    wide = math.gcd(tiles, STEP // LANES)
    step = wide * LANES
    per = tiles // wide
    half = 2 * chans * TS
    last = shards * per
    ways = math.gcd(last, WAYS)
    if ways < last:
        sides[-1][...] = jnp.zeros_like(sides[-1])

    def part(t):
        row = (t % per if isinstance(t, int) else lax.rem(t, per)) * (wide * COORD_ROWS)
        rows = [pl.ds(row + n * COORD_ROWS if isinstance(t, int) else pl.multiple_of(row + n * COORD_ROWS, COORD_ROWS), COORD_ROWS) for n in range(wide)]
        return jnp.concatenate([so_ref[t // per, at] for at in rows], 1)

    def product(t, into):
        made = source_rows(part(t), directions, depth)
        into[...] = jnp.dot(lhs[...], made, preferred_element_type=jnp.float32)

    def phasors(t, both, sides):
        src = part(t)
        kinds = jnp.broadcast_to(src[3:4].astype(jnp.int32), (TS, step))
        for side in range(2):
            for c in range(chans):
                at = (side * chans + c) * TS
                turns = both[at : at + TS]
                if side == 0:
                    size = both[half + at : half + at + TS] * src[4 + c : 5 + c]
                else:
                    table = sizes[c * TS : (c + 1) * TS]
                    size = jnp.concatenate([look_up(table, kinds[:, n : n + LANES]) for n in range(0, step, LANES)], 1)
                re, im = phasor(turns, size)
                sides[2 * at : 2 * at + TS] = re.astype(jnp.bfloat16)
                sides[2 * at + TS : 2 * at + 2 * TS] = im.astype(jnp.bfloat16)

    def collect(sides):
        whole = lax.dot_general(
            sides[:half], sides[half:], (((1,), (1,)), ((), ())), preferred_element_type=jnp.float32
        )
        for at in range(0, half, LANES):
            total[at : at + LANES] += whole[at : at + LANES, at : at + LANES]

    product(0, both[0])

    def turn(t, carry):
        for way in range(ways):
            at = t * ways + way
            product(jnp.minimum(at + 1, last - 1), both[(way + 1) % 2])
            phasors(at, both[way % 2], sides[way % 2])
            collect(sides[(way + 1) % 2])
        return carry

    if ways < last:
        lax.fori_loop(0, last // ways, turn, 0)
    else:
        for at in range(last):
            if at + 1 < last:
                product(at + 1, both[(at + 1) % 2])
            phasors(at, both[at % 2], sides[at % 2])
            if at:
                collect(sides[(at + 1) % 2])
    collect(sides[(last - 1) % 2])


def first_kernel(chans, directions, depth, row, size, pairs_ref, st0, st1, so_ref, lhs, sizes, total, *work):
    total[...] = jnp.zeros_like(total)
    if row is not None:
        me = lax.axis_index("src")
        pair = place(pairs_ref[pl.ds(me * row[0] + row[1], 1)] ^ me, size)
    for side in range(2):
        if row is None:
            block = st0[side]
        else:
            at = jnp.broadcast_to(pair[:, side : side + 1], st0.shape[1:])
            block = jnp.zeros(st0.shape[1:], jnp.float32)
            for n in range(st0.shape[0]):
                block = jnp.where(at == n, st0[n], block)
                block = jnp.where(at == n + st0.shape[0], st1[n], block)
        phase, amplitude, size = station_rows(block, directions, depth)
        lhs[side * LANES : (side + 1) * LANES] = phase
        if side == 0:
            lhs[2 * LANES : 3 * LANES] = amplitude
        else:
            sizes[...] = size
    add_sources(chans, directions, depth, so_ref, lhs, sizes, total, *work)


def next_kernel(chans, directions, depth, lhs, sizes, before, so_ref, total, *work):
    total[...] = before[...]
    add_sources(chans, directions, depth, so_ref, lhs, sizes, total, *work)


def last_kernel(chans, directions, depth, row, pairs_ref, lhs, sizes, before, so_ref, out_ref, total, *work):
    total[...] = before[...]
    add_sources(chans, directions, depth, so_ref, lhs, sizes, total, *work)
    me = lax.axis_index("src") * row[0] + row[1]
    pair = pairs_ref[pl.ds(me, 1)]
    same = pair[:, 0:1] == pair[:, 1:2]
    high = lax.broadcasted_iota(jnp.int32, (8, LANES), 0)
    lane = lax.broadcasted_iota(jnp.int32, (8, LANES), 1)
    fold = LANES // TS
    clear = jnp.logical_and(lane % TS == high * fold + lane // TS, same)
    for c in range(chans):
        base = 2 * c * TS
        column = base % LANES
        real = jnp.zeros((8, LANES), jnp.float32)
        imag = jnp.zeros((8, LANES), jnp.float32)
        for b in range(fold):
            w_re = total[pl.ds(base + b, 8, stride=fold)]
            w_im = total[pl.ds(base + TS + b, 8, stride=fold)]
            here = lane // TS == b
            one = (b * TS - column) % LANES
            two = (b * TS - column - TS) % LANES
            real = jnp.where(here, pltpu.roll(w_re, one, 1) + pltpu.roll(w_im, two, 1), real)
            imag = jnp.where(here, pltpu.roll(w_im, one, 1) - pltpu.roll(w_re, two, 1), imag)
        for n, values in enumerate((real, imag)):
            values = jnp.where(clear, 0.0, values)
            for m in range(8):
                out_ref[c, n : n + 1, m * LANES : (m + 1) * LANES] = values[m : m + 1]


class Predictor:
    def __init__(self, chans, directions, width):
        self.chans, self.directions = chans, directions
        self.depth = -(-(SOURCE_ROWS + 3 * directions) // LANES) * LANES
        step = math.gcd(width, STEP)
        self.work = [pltpu.VMEM((3 * chans * TS, step), jnp.float32)] * 2
        self.work += [pltpu.VMEM((4 * chans * TS, step), jnp.bfloat16)] * 2
        self.total = (2 * chans * TS, LANES)

    def call(self, kernel, out_shape, scratch, args):
        vmem = pl.BlockSpec(memory_space=pltpu.VMEM)
        sources = args[-1].size // COORD_ROWS
        count = 2 * self.chans * TS * sources
        return pl.pallas_call(
            kernel,
            out_shape=out_shape,
            in_specs=[vmem] * len(args),
            out_specs=jax.tree.map(lambda _: vmem, out_shape),
            scratch_shapes=scratch,
            compiler_params=pltpu.CompilerParams(vmem_limit_bytes=32 << 20),
            cost_estimate=pl.CostEstimate(flops=2000 * count, bytes_accessed=0, transcendentals=count),
        )(*args)

    def first(self, row, size, pairs, stations, sources):
        kernel = functools.partial(first_kernel, self.chans, self.directions, self.depth, row, size)
        shapes = (
            jax.ShapeDtypeStruct((3 * LANES, self.depth), jnp.bfloat16),
            jax.ShapeDtypeStruct((LANES, LANES), jnp.float32),
            jax.ShapeDtypeStruct(self.total, jnp.float32),
        )
        return self.call(kernel, shapes, self.work, (pairs, *stations, sources))

    def next(self, lhs, sizes, total, sources):
        kernel = functools.partial(next_kernel, self.chans, self.directions, self.depth)
        shape = jax.ShapeDtypeStruct(self.total, jnp.float32)
        return self.call(kernel, shape, self.work, (lhs, sizes, total, sources))

    def last(self, row, pairs, lhs, sizes, total, sources):
        kernel = functools.partial(last_kernel, self.chans, self.directions, self.depth, row)
        shape = jax.ShapeDtypeStruct((self.chans, 2, TS * TS), jnp.float32)
        scratch = [pltpu.VMEM(self.total, jnp.float32)] + self.work
        return self.call(kernel, shape, scratch, (pairs, lhs, sizes, total, sources))


def pack_kernel(scale, chans, channel_ref, positions_ref, flux_ref, cluster_ref, jones_ref, uvw_ref, station_ref, source_ref):
    own = uvw_ref.shape[1]
    directions = jones_ref.shape[2]
    coords = positions_ref[...]
    l_term, m_term = coords[0:1], coords[1:2]
    n_term = jnp.sqrt(1.0 - l_term * l_term - m_term * m_term) - 1.0
    kinds = cluster_ref[...].astype(jnp.float32)
    source = jnp.concatenate([coords, n_term, kinds, flux_ref[...] * scale], 0)
    for n in range(coords.shape[1] // LANES):
        source_ref[0, n * COORD_ROWS : (n + 1) * COORD_ROWS] = source[:, n * LANES : (n + 1) * LANES]
    station_ref[...] = jnp.zeros_like(station_ref)
    for c in range(chans):
        lanes = slice(c * own, (c + 1) * own)
        ratio = 1.0 + 0.002 * channel_ref[c].astype(jnp.float32)
        station_ref[0, 0:3, lanes] = uvw_ref[...] * ratio
        for n in range(2):
            begin = COORD_ROWS + n * directions
            station_ref[0, begin : begin + directions, lanes] = jones_ref[c, n]


def pack(positions, flux, cluster, jones, station_uvw, channels, scale):
    chans, _, directions, own = jones.shape
    vmem = pl.BlockSpec(memory_space=pltpu.VMEM)
    return pl.pallas_call(
        functools.partial(pack_kernel, scale, chans),
        out_shape=(
            jax.ShapeDtypeStruct((1, COORD_ROWS + 2 * directions, chans * own), jnp.float32),
            jax.ShapeDtypeStruct((1, positions.shape[1] // LANES * COORD_ROWS, LANES), jnp.float32),
        ),
        in_specs=[pl.BlockSpec(memory_space=pltpu.SMEM)] + [vmem] * 5,
        out_specs=(vmem, vmem),
    )(channels, positions, flux, cluster[None], jones, station_uvw)


def swap(x, bit, size):
    return lax.ppermute(x, "src", [(i, i ^ bit) for i in range(size)])


def after(x, *earlier):
    return lax.optimization_barrier((x, *earlier))[0]


def spread(station, source, size):
    bit, arrived = size // 2, None
    while bit > 4:
        ready = source if arrived is None else after(source, arrived)
        arrived = swap(station, bit, size)
        source = jnp.concatenate([source, swap(ready, bit, size)], 0)
        station = jnp.concatenate([station, arrived], 0)
        bit //= 2
    arrived = swap(station, 4, size)
    station = jnp.concatenate([station, arrived], 0)
    ready = after(source, arrived)
    station = jnp.concatenate([station, swap(station, 2, size)], 0)
    across = swap(ready, 2, size)
    other = swap(ready, 4, size)
    across = jnp.concatenate([across, swap(other, 2, size)], 0)
    return (station, swap(station, 1, size)), jnp.concatenate([source, other], 0), across


def on_device(positions, flux, cluster, jones, station_uvw, channels, tile_map):
    size = lax.axis_size("src")
    chans, _, directions, own = jones.shape
    scale = 1.0 / math.sqrt(positions.shape[1] * size)
    station, source = pack(positions, flux, cluster, jones, station_uvw, channels, scale)
    stations, source, got = spread(station, source, size)
    own_rows = tile_map.shape[0] // size
    many = TS // own
    predictor = Predictor(chans, directions, positions.shape[1])
    begun = []
    for row in range(own_rows):
        if many == 1:
            begun.append(predictor.first((own_rows, row), size, tile_map, stations, source))
        else:
            me = lax.axis_index("src")
            pair = lax.dynamic_slice_in_dim(tile_map, me * own_rows + row, 1, 0)[0]
            whole = jnp.concatenate(stations, 0)
            of = place((pair[:, None] * many + jnp.arange(many)[None, :]) ^ me, size)
            picked = jnp.take(whole, of.reshape(-1), axis=0)
            picked = picked.reshape(2, many, whole.shape[1], chans, own)
            picked = jnp.transpose(picked, (0, 2, 3, 1, 4)).reshape(2, whole.shape[1], chans * TS)
            begun.append(predictor.first(None, size, tile_map, (picked, picked), source))
    both = jnp.concatenate([after(source, begun[-1][-1]), got], 0)
    other = swap(both, 1, size)
    out = []
    for row, (lhs, sizes, total) in enumerate(begun):
        total = predictor.next(lhs, sizes, total, got)
        out.append(predictor.last((own_rows, row), tile_map, lhs, sizes, total, other))
    return jnp.stack(out)


def solution(mesh):
    in_specs = (
        P(None, ("group", "src")),
        P(None, ("group", "src")),
        P(("group", "src")),
        P(None, None, None, ("group", "src")),
        P(None, ("group", "src")),
        P("group"),
        P("group", None),
    )
    out_specs = P(("group", "src"), None, None, None)
    return jax.shard_map(
        on_device, mesh=mesh, in_specs=in_specs, out_specs=out_specs, check_vma=False
    )
```
